512 devices in a mesh: dap: 64 (over y, z_lo, core), ch: 8 (over x, z_hi).
Axes of the slice: x: 4, y: 8, z: 8 (z_hi: 2, z_lo: 4; z = z_hi * 4 + z_lo), core: 2. Of those that a mesh axis runs over, the one named last changes fastest.
Arguments:
- pair: bfloat16 [128, 512, 512], P('ch', 'dap'), may hold values from -25 to 25
- pair_mask: int32 [512, 512], P('dap'), may hold values 0 or 1
- in_gain: float32 [128], replicated, may hold values from 0.1 to 1.9
- in_bias: float32 [128], replicated, may hold values from -3 to 3
- ab_weight: bfloat16 [4, 128, 128], P(None, None, 'ch'), may hold values from -2 to 2
- hid_gain: float32 [128], P('ch'), may hold values from 0.1 to 1.9
- hid_bias: float32 [128], P('ch'), may hold values from -3 to 3
- out_weight: bfloat16 [128, 128], P('ch'), may hold values from -0.5 to 0.5
- gate_weight: bfloat16 [128, 128], P(None, 'ch'), may hold values from -0.5 to 0.5
Outputs:
- update_t: bfloat16 [128, 512, 512], P('ch', 'dap')
The draws below stay inside these ranges and needn't reach their ends.
All inputs are finite; a program needn't handle non-finite values. No bound on the sum of `pair_mask` on one device may be relied on, other than what follows from the above.
Results may differ from the reference program's by a relative error of at most 0.0055.
Values may be sent and summed in bfloat16 or wider, within the bound.
A program may use at most 64 MiB of HBM per device.

```python
import jax
import jax.numpy as jnp
from jax import lax

PAIR_CH = 128
TRI_CH = 128
RESIDUES = 512


def draw_pair(key, part):
    key = jax.random.fold_in(key, 3)
    first = jax.random.fold_in(key, 0)
    rising = 3.0 ** (jnp.arange(PAIR_CH, dtype=jnp.float32) / (PAIR_CH - 1))
    values = jnp.clip(jax.random.normal(first, (PAIR_CH, RESIDUES, RESIDUES), jnp.float32), -6.0, 6.0)
    return (values * rising[:, None, None]).astype(jnp.bfloat16)


def draw_ab_weight(key, part):
    key = jax.random.fold_in(key, 5)
    rising = 3.0 ** (0.5 * jnp.arange(TRI_CH, dtype=jnp.float32) / (TRI_CH - 1))
    flat_ones = jnp.ones((TRI_CH,), jnp.float32)
    factor = jnp.stack([flat_ones, rising, flat_ones, rising])[:, None, :]
    base = jnp.clip(jax.random.normal(key, (4, PAIR_CH, TRI_CH), jnp.float32), -4.0, 4.0)
    return (base * PAIR_CH ** (-0.5) * factor).astype(jnp.bfloat16)


def set_ends(drawn, key, least, largest):
    shape = drawn.shape
    place = [jax.random.randint(jax.random.fold_in(key, axis), (), 0, shape[axis]) for axis in range(len(shape))]
    drawn = drawn.at[tuple(place)].set(least)
    longest = shape.index(max(shape))
    place[longest] = (place[longest] + 1) % shape[longest]
    return drawn.at[tuple(place)].set(largest)


def level_of(rng, shape, shards, least, high):
    factor_of, own = 1.0, jax.random.fold_in(rng, 6)
    for axis_at, parts in shards:
        draws = jnp.exp(jax.random.uniform(jax.random.fold_in(own, axis_at), (parts,), jnp.float32, least / len(shards), high / len(shards)))
        factor_of = factor_of * jnp.repeat(draws, shape[axis_at] // parts).reshape([-1 if axis == axis_at else 1 for axis in range(len(shape))])
    return factor_of


def gaussian(rng, shape, deviation, limit, shards=(), kind=jnp.bfloat16):
    values = deviation * jax.random.normal(rng, shape, jnp.float32)
    if shards:
        values = values * level_of(rng, shape, shards, -0.22, 0.18)
    return jnp.clip(values, -limit, limit).astype(kind)


def setup_inputs(seed: int = 0) -> dict:
    key_of = jax.random.split(jax.random.key(seed), 10)
    pair = draw_pair(jax.random.fold_in(key_of[9], 71), 0)
    pair_mask = set_ends((jax.random.randint(key_of[1], (RESIDUES, RESIDUES), 0, 8) < 7).astype(jnp.int32), jax.random.fold_in(key_of[1], 1), 0, 1)
    in_gain = jnp.clip(1.0 + 0.18 * jax.random.normal(key_of[2], (PAIR_CH,), jnp.float32), 0.1, 1.9)
    in_bias = gaussian(key_of[3], (PAIR_CH,), 0.5, 3.0, (), jnp.float32)
    ab_weight = draw_ab_weight(jax.random.fold_in(key_of[9], 71), 0)
    hid_gain = jnp.clip(1.0 + 0.18 * jax.random.normal(key_of[5], (TRI_CH,), jnp.float32), 0.1, 1.9)
    hid_bias = gaussian(key_of[6], (TRI_CH,), 0.5, 3.0, ((0, 8),), jnp.float32)
    out_weight = gaussian(key_of[7], (TRI_CH, PAIR_CH), TRI_CH ** -0.5, 0.5, ((0, 8),))
    gate_weight = gaussian(key_of[8], (PAIR_CH, PAIR_CH), PAIR_CH ** -0.5, 0.5, ((1, 8),))
    return {"pair": pair, "pair_mask": pair_mask, "in_gain": in_gain, "in_bias": in_bias, "ab_weight": ab_weight, "hid_gain": hid_gain, "hid_bias": hid_bias, "out_weight": out_weight, "gate_weight": gate_weight}


EPS = 1e-05

def layer_norm(values, gain, bias):
    mean = lax.optimization_barrier(jnp.mean(values, 0))
    square = lax.optimization_barrier(jnp.mean(values * values, 0))
    var = square - mean * mean
    return (values - mean) * lax.rsqrt(var + EPS) * gain[:, None, None] + bias[:, None, None]

def reference(pair, pair_mask, in_gain, in_bias, ab_weight, hid_gain, hid_bias, out_weight, gate_weight):
    z_ln = layer_norm(pair.astype(jnp.float32), in_gain, in_bias).astype(jnp.bfloat16)
    flat = z_ln.reshape(PAIR_CH, RESIDUES * RESIDUES)
    masking = pair_mask.astype(jnp.float32).reshape(-1)

    def project(index):
        return jnp.dot(ab_weight[index].T, flat, preferred_element_type=jnp.float32)
    left = (jax.nn.sigmoid(project(0)) * project(1) * masking).astype(jnp.bfloat16)
    right = (jax.nn.sigmoid(project(2)) * project(3) * masking).astype(jnp.bfloat16)
    left = left.reshape(TRI_CH, RESIDUES, RESIDUES).astype(jnp.float32)
    right = right.reshape(TRI_CH, RESIDUES, RESIDUES).astype(jnp.float32)
    tri = jnp.einsum('hik,hjk->hij', left, right)
    tri_ln = layer_norm(tri, hid_gain, hid_bias).astype(jnp.bfloat16)
    proj_out = jnp.dot(out_weight.T, tri_ln.reshape(TRI_CH, -1), preferred_element_type=jnp.float32)
    gate = jax.nn.sigmoid(jnp.dot(gate_weight.T, flat, preferred_element_type=jnp.float32))
    update = (gate * proj_out).reshape(PAIR_CH, RESIDUES, RESIDUES).astype(jnp.bfloat16)
    return jnp.swapaxes(update, 1, 2)
```

```python
import jax
import jax.numpy as jnp
from jax import lax
from jax.experimental import pallas as pl
from jax.experimental.pallas import tpu as pltpu
from jax.sharding import PartitionSpec as P

CH = 128
RES = 512
EPS = 1e-05
MESH = pl.DeviceIdType.MESH
F32 = jnp.float32
BF16 = jnp.bfloat16


def nt(a, b):
    return lax.dot_general(a, b, (((1,), (1,)), ((), ())), preferred_element_type=F32)


def nn(a, b):
    return lax.dot_general(a, b, (((1,), (0,)), ((), ())), preferred_element_type=F32)


def iota(shape, dim):
    return lax.broadcasted_iota(jnp.int32, shape, dim)


def sigmoid(x):
    return 1.0 / (1.0 + jnp.exp(-x))


def norm(values, gain, bias):
    mean = jnp.sum(values, 0, keepdims=True) * (1.0 / CH)
    square = jnp.sum(values * values, 0, keepdims=True) * (1.0 / CH)
    var = square - mean * mean
    return (values - mean) * lax.rsqrt(var + EPS) * gain + bias


def kernel(pair, mask, gain, bias, ab, hid_gain, hid_bias, out_weight, gate_weight, out,
           work, zsend, zrecv, wasend, warecv, wbsend, wbrecv, hsend, hrecv,
           lrsend, lrrecv, rows, lbuf, rbuf, tsend, t1, t2send, t2, gsend, g1, g2send, g2, usend,
           ssem, rsem):
    dap = lax.axis_index("dap")
    ch = lax.axis_index("ch")
    p = lax.div(dap, 2)
    core = lax.rem(dap, 2)
    q = core * 8 + ch
    y = lax.div(p, 4)
    z = lax.rem(p, 4)
    zh = lax.div(z, 2)
    zl = lax.rem(z, 2)

    def dev_q(q2):
        return (p * 2 + lax.div(q2, 8), lax.rem(q2, 8))

    def dev_p(p2):
        return (p2 * 2 + core, ch)

    def each(first, last, body):
        def step(k, carry):
            body(k)
            return carry
        lax.fori_loop(first, last, step, 0)

    def send(src, dst, sem, device):
        pltpu.make_async_remote_copy(
            src_ref=src, dst_ref=dst, send_sem=ssem.at[sem], recv_sem=rsem.at[sem],
            device_id=device, device_id_type=MESH).start()

    def wait_in(ref, sem):
        pltpu.make_async_copy(ref, ref, rsem.at[sem]).wait()

    def wait_out(ref, sem):
        pltpu.make_async_copy(ref, ref, ssem.at[sem]).wait()

    barrier = pltpu.get_barrier_semaphore()

    def greet_q(k):
        pl.semaphore_signal(barrier, inc=1, device_id=dev_q(lax.rem(q + k, 16)), device_id_type=MESH)

    def greet_p(k):
        pl.semaphore_signal(barrier, inc=1, device_id=dev_p(lax.rem(p + k, 32)), device_id_type=MESH)

    each(1, 16, greet_q)
    each(1, 32, greet_p)

    for kc in range(4):
        lanes = pl.ds(kc * 128, 128)
        work[kc, pl.ds(0, 128), :] = pair[:, :, lanes].astype(F32).reshape(128, 128)
    for kc in range(4):
        lanes = pl.ds(kc * 128, 128)
        for r in range(8):
            zsend[r, :, lanes] = work[kc, pl.ds(r, 16, stride=8), :].astype(BF16)
    eye16 = (iota((16, 16), 0) == iota((16, 16), 1)).astype(BF16)
    for m in range(4):
        wasend[pl.ds(m * 16, 16), :] = nt(eye16, ab[m]).astype(BF16)
    wbsend[pl.ds(0, 16), :] = nt(eye16, gate_weight[...]).astype(BF16)
    wbsend[pl.ds(16, 16), :] = out_weight[...]
    hsend[...] = jnp.zeros((8, 128), F32)
    hsend[pl.ds(0, 1), pl.ds(0, 16)] = hid_gain[...]
    hsend[pl.ds(1, 1), pl.ds(0, 16)] = hid_bias[...]

    pl.semaphore_wait(barrier, 46)

    def peer(k):
        return lax.rem(ch + k, 8)

    each(1, 8, lambda k: send(zsend.at[peer(k)], zrecv.at[ch], 0, (dap, peer(k))))
    each(1, 8, lambda k: send(wasend, warecv.at[ch], 1, (dap, peer(k))))
    each(1, 8, lambda k: send(wbsend, wbrecv.at[ch], 2, (dap, peer(k))))
    each(1, 8, lambda k: send(hsend, hrecv.at[ch], 3, (dap, peer(k))))
    zrecv[ch] = zsend[ch]
    warecv[ch] = wasend[...]
    wbrecv[ch] = wbsend[...]
    hrecv[ch] = hsend[...]

    eye = iota((128, 128), 0) == iota((128, 128), 1)
    gain_col = jnp.sum(jnp.where(eye, gain[...], 0.0), 1, keepdims=True)
    bias_col = jnp.sum(jnp.where(eye, bias[...], 0.0), 1, keepdims=True)
    masking = mask[pl.ds(ch, 1), :].astype(F32)

    wait_in(zrecv.at[pl.ds(0, 7)], 0)
    zn = norm(zrecv[...].astype(F32).reshape(128, RES), gain_col, bias_col).astype(BF16)
    wait_in(warecv.at[pl.ds(0, 7)], 1)

    def project(m):
        weight = warecv[:, pl.ds(m * 16, 16), :].reshape(128, 128)
        return nn(weight, zn)

    left = (sigmoid(project(0)) * project(1) * masking).reshape(16, 8, RES)
    right = (sigmoid(project(2)) * project(3) * masking).reshape(16, 8, RES)
    lrsend[...] = jnp.concatenate([left, right], axis=1).astype(BF16)

    def other_q(k):
        return lax.rem(q + k, 16)

    each(1, 16, lambda k: send(lrsend.at[other_q(k)], lrrecv.at[q], 4, dev_q(other_q(k))))
    lrrecv[q] = lrsend[q]

    wait_in(wbrecv.at[pl.ds(0, 7)], 2)
    gate = sigmoid(nn(wbrecv[:, pl.ds(0, 16), :].reshape(128, 128), zn))
    gsend[...] = gate.T.astype(BF16).reshape(32, 16, 128)

    def other_p(k):
        return lax.rem(p + k, 32)

    each(1, 32, lambda k: send(gsend.at[other_p(k)], g1.at[p], 5, dev_p(other_p(k))))
    g1[p] = gsend[p]
    wout_t = nt(eye.astype(BF16), wbrecv[:, pl.ds(16, 16), :].reshape(128, 128)).astype(BF16)

    wait_in(lrrecv.at[pl.ds(0, 15)], 4)
    for kc in range(4):
        work[kc, :, :] = lrrecv[:, :, pl.ds(kc * 128, 128)].astype(F32).reshape(256, 128)
    for t in range(16):
        for kc in range(4):
            rows[t, :, pl.ds(kc * 128, 128)] = work[kc, pl.ds(t, 16, stride=16), :].astype(BF16)

    lslot = y * 2 + zl
    rslot = y * 2 + zh
    lpair = zh * 2 + (1 - zl)
    rpair = (1 - zh) * 2 + zl

    send(rows.at[y], lbuf.at[lslot], 6, dev_p(y * 4 + lpair))
    send(rows.at[8 + y], rbuf.at[rslot], 11, dev_p(y * 4 + rpair))

    def share(k):
        h = lax.rem(y + k, 8)
        send(rows.at[h], lbuf.at[lslot], 6, dev_p(h * 4 + z))
        send(rows.at[8 + h], rbuf.at[rslot], 11, dev_p(h * 4 + z))
        send(rows.at[h], lbuf.at[lslot], 6, dev_p(h * 4 + lpair))
        send(rows.at[8 + h], rbuf.at[rslot], 11, dev_p(h * 4 + rpair))

    each(1, 8, share)
    lbuf[lslot] = rows[y]
    rbuf[rslot] = rows[8 + y]

    wait_in(g1.at[pl.ds(0, 31)], 5)
    work[0, :, :] = g1[pl.ds(0, 16)].astype(F32).reshape(256, 128)
    work[1, :, :] = g1[pl.ds(16, 16)].astype(F32).reshape(256, 128)
    for j in range(16):
        for half in range(2):
            g2send[j, pl.ds(half * 16, 16), :] = work[half, pl.ds(j, 16, stride=16), :].astype(BF16)
    each(1, 16, lambda k: send(g2send.at[other_q(k)], g2.at[q], 7, dev_q(other_q(k))))
    g2[q] = g2send[q]

    wait_in(lbuf.at[pl.ds(0, 15)], 6)
    wait_in(rbuf.at[pl.ds(0, 15)], 11)
    tri = nt(rbuf[...].reshape(256, RES), lbuf[...].reshape(256, RES))
    tsend[...] = tri.astype(BF16).reshape(16, 16, 256)
    tslot = zh * 8 + y

    def back(k):
        b = lax.rem(rslot + k, 16)
        send(tsend.at[b], t1.at[tslot], 8, dev_p(lax.div(b, 2) * 4 + lax.rem(b, 2) * 2 + zl))

    each(1, 16, back)
    t1[tslot] = tsend[rslot]

    wait_in(t1.at[pl.ds(0, 15)], 8)
    for kc in range(2):
        work[kc, :, :] = t1[:, :, pl.ds(kc * 128, 128)].astype(F32).reshape(256, 128)
    for j in range(16):
        for kc in range(2):
            t2send[j, :, pl.ds(kc * 128, 128)] = work[kc, pl.ds(j, 16, stride=16), :].astype(BF16)
    each(1, 16, lambda k: send(t2send.at[other_q(k)], t2.at[q], 9, dev_q(other_q(k))))
    t2[q] = t2send[q]

    wait_in(g2.at[pl.ds(0, 15)], 7)
    work[2, :, :] = g2[pl.ds(0, 8)].astype(F32).reshape(256, 128)
    work[3, :, :] = g2[pl.ds(8, 8)].astype(F32).reshape(256, 128)
    pieces = []
    for zhi in range(2):
        for yy in range(8):
            for zlo in range(2):
                at = yy * 4 + zhi * 2 + zlo
                pieces.append(work[2, pl.ds(at, 8, stride=32), :])
                pieces.append(work[3, pl.ds(at, 8, stride=32), :])
    gate_t = jnp.concatenate(pieces, axis=0).T
    wait_in(hrecv.at[pl.ds(0, 7)], 3)
    at_lane = (iota((8, 16, 128), 1) == iota((8, 16, 128), 2))
    hg_col = jnp.sum(jnp.where(at_lane, hrecv[:, pl.ds(0, 1), :], 0.0), 2, keepdims=True).reshape(128, 1)
    hb_col = jnp.sum(jnp.where(at_lane, hrecv[:, pl.ds(1, 1), :], 0.0), 2, keepdims=True).reshape(128, 1)
    lane = iota((RES, RES), 0)
    natural = lax.rem(lane, 256) // 32 * 64 + lane // 256 * 32 + lax.rem(lane, 32)
    perm = (natural == iota((RES, RES), 1)).astype(BF16)

    wait_in(t2.at[pl.ds(0, 15)], 9)
    tri = t2[...].astype(F32).reshape(16, 2, 8, 256)
    tri = jnp.concatenate([tri[:, 0].reshape(128, 256), tri[:, 1].reshape(128, 256)], axis=1)
    tri_ln = norm(tri, hg_col, hb_col).astype(BF16)
    update = (nn(wout_t, tri_ln) * gate_t).astype(BF16)
    usend[...] = nn(update, perm).astype(BF16).reshape(8, 16, RES)
    each(1, 8, lambda k: send(usend.at[peer(k)], out.at[ch], 10, (dap, peer(k))))
    out[ch] = usend[ch]

    wait_out(zsend.at[pl.ds(0, 7)], 0)
    wait_out(warecv.at[pl.ds(0, 7)], 1)
    wait_out(wbrecv.at[pl.ds(0, 7)], 2)
    wait_out(hrecv.at[pl.ds(0, 7)], 3)
    wait_out(lrsend.at[pl.ds(0, 15)], 4)
    wait_out(gsend.at[pl.ds(0, 31)], 5)
    wait_out(rows.at[pl.ds(0, 15)], 6)
    wait_out(rows.at[pl.ds(0, 15)], 11)
    wait_out(g2send.at[pl.ds(0, 15)], 7)
    wait_out(tsend.at[pl.ds(0, 15)], 8)
    wait_out(t2send.at[pl.ds(0, 15)], 9)
    wait_out(usend.at[pl.ds(0, 7)], 10)
    wait_in(out.at[pl.ds(0, 7)], 10)


def body(pair, pair_mask, in_gain, in_bias, ab_weight, hid_gain, hid_bias, out_weight, gate_weight):
    vmem = pl.BlockSpec(memory_space=pltpu.VMEM)
    swapped = pl.pallas_call(
        kernel,
        out_shape=jax.ShapeDtypeStruct((8, 16, RES), BF16),
        in_specs=[vmem] * 9,
        out_specs=vmem,
        scratch_shapes=[
            pltpu.VMEM((4, 256, 128), F32),
            pltpu.VMEM((8, 16, RES), BF16),
            pltpu.VMEM((8, 16, RES), BF16),
            pltpu.VMEM((64, 128), BF16),
            pltpu.VMEM((8, 64, 128), BF16),
            pltpu.VMEM((32, 128), BF16),
            pltpu.VMEM((8, 32, 128), BF16),
            pltpu.VMEM((8, 128), F32),
            pltpu.VMEM((8, 8, 128), F32),
            pltpu.VMEM((16, 16, RES), BF16),
            pltpu.VMEM((16, 16, RES), BF16),
            pltpu.VMEM((16, 16, RES), BF16),
            pltpu.VMEM((16, 16, RES), BF16),
            pltpu.VMEM((16, 16, RES), BF16),
            pltpu.VMEM((16, 16, 256), BF16),
            pltpu.VMEM((16, 16, 256), BF16),
            pltpu.VMEM((16, 16, 256), BF16),
            pltpu.VMEM((16, 16, 256), BF16),
            pltpu.VMEM((32, 16, 128), BF16),
            pltpu.VMEM((32, 16, 128), BF16),
            pltpu.VMEM((16, 32, 128), BF16),
            pltpu.VMEM((16, 32, 128), BF16),
            pltpu.VMEM((8, 16, RES), BF16),
            pltpu.SemaphoreType.DMA((12,)),
            pltpu.SemaphoreType.DMA((12,)),
        ],
        compiler_params=pltpu.CompilerParams(
            collective_id=0, has_side_effects=True, vmem_limit_bytes=32 * 1024 * 1024),
    )(pair, pair_mask, in_gain.reshape(1, CH), in_bias.reshape(1, CH), ab_weight,
      hid_gain.reshape(1, 16), hid_bias.reshape(1, 16), out_weight, gate_weight)
    return jnp.swapaxes(swapped, 0, 1)


def solution(mesh):
    placed = (
        P("ch", "dap", None),
        P("dap", None),
        P(),
        P(),
        P(None, None, "ch"),
        P("ch"),
        P("ch"),
        P("ch", None),
        P(None, "ch"),
    )
    return jax.shard_map(
        body, mesh=mesh, in_specs=placed, out_specs=P("ch", "dap", None), check_vma=False
    )
```

```python
import jax
import jax.numpy as jnp
from jax import lax
from jax.experimental import pallas as pl
from jax.experimental.pallas import tpu as pltpu
from jax.sharding import PartitionSpec as P

CH = 128
RES = 512
EPS = 1e-05
MESH = pl.DeviceIdType.MESH
F32 = jnp.float32
BF16 = jnp.bfloat16


def nt(a, b):
    return lax.dot_general(a, b, (((1,), (1,)), ((), ())), preferred_element_type=F32)


def nn(a, b):
    return lax.dot_general(a, b, (((1,), (0,)), ((), ())), preferred_element_type=F32)


def iota(shape, dim):
    return lax.broadcasted_iota(jnp.int32, shape, dim)


def bits(value, low, count):
    return lax.shift_right_logical(value, low) & ((1 << count) - 1)


def sigmoid(x):
    return 1.0 / (1.0 + jnp.exp(-x))


def norm(values, gain, bias):
    mean = jnp.sum(values, 0, keepdims=True) * (1.0 / CH)
    square = jnp.sum(values * values, 0, keepdims=True) * (1.0 / CH)
    var = square - mean * mean
    return (values - mean) * lax.rsqrt(var + EPS) * gain + bias


def each(first, last, body):
    def step(k, carry):
        body(k)
        return carry
    lax.fori_loop(first, last, step, 0)


def kernel(pair, mask, gain, bias, ab, hid_gain, hid_bias, out_weight, gate_weight, out,
           work, zsend, zrecv, wasend, warecv, wbsend, wbrecv, hsend, hrecv, msend, mrecv,
           lrsend, lrrecv, rows, lbuf, rbuf, tsend, t1, t2send, t2, gsend, g1, g2send, g2, usend,
           ssem, rsem):
    div, rem = lax.div, lax.rem
    dap = lax.axis_index("dap")
    ch = lax.axis_index("ch")
    x, z_hi = div(ch, 2), rem(ch, 2)
    y, z_lo, core = div(dap, 8), rem(div(dap, 2), 4), rem(dap, 2)
    z = z_hi * 4 + z_lo
    b = y * 2 + core
    e_lo, e_ch = rem(z + 2, 4), 2 * x + div(rem(z + 6, 8), 4)
    e = e_lo * 8 + e_ch
    half, quarter = div(y, 4), rem(y, 4)

    def place(x2, z2):
        return ((y * 4 + rem(z2, 4)) * 2 + core, x2 * 2 + div(z2, 4))

    def dev_e(e2):
        return place(div(rem(e2, 8), 2), rem(div(e2, 8) + 2 + 4 * rem(e2, 2), 8))

    def dev_b(b2):
        return ((div(b2, 2) * 4 + z_lo) * 2 + rem(b2, 2), ch)

    def send(src, dst, sem, device):
        pltpu.make_async_remote_copy(
            src_ref=src, dst_ref=dst, send_sem=ssem.at[sem], recv_sem=rsem.at[sem],
            device_id=device, device_id_type=MESH).start()

    def wait_in(ref, sem):
        pltpu.make_async_copy(ref, ref, rsem.at[sem]).wait()

    def wait_out(ref, sem):
        pltpu.make_async_copy(ref, ref, ssem.at[sem]).wait()

    barrier = pltpu.get_barrier_semaphore()

    def greet(device):
        pl.semaphore_signal(barrier, inc=1, device_id=device, device_id_type=MESH)

    def greet_near(k):
        greet(place(rem(x + div(k, 5), 4), rem(z + 6 + rem(k + 2, 5), 8)))

    each(1, 16, lambda k: greet(dev_b(rem(b + k, 16))))
    each(1, 20, greet_near)

    for kc in range(4):
        work[kc, pl.ds(0, 128), :] = pair[:, :, pl.ds(kc * 128, 128)].astype(F32).reshape(128, 128)
    for kc in range(4):
        for r in range(8):
            zsend[r, :, pl.ds(kc * 128, 128)] = work[kc, pl.ds(r, 16, stride=8), :].astype(BF16)
    own_mask = mask[pl.ds(ch, 1), :].astype(F32)
    for kc in range(4):
        msend[pl.ds(kc, 1), :] = own_mask[:, kc * 128:kc * 128 + 128]

    pl.semaphore_wait(barrier, 34)

    each(0, 8, lambda k: send(zsend.at[rem(ch + k, 8)], zrecv.at[ch], 0, dev_e(z_lo * 8 + rem(ch + k, 8))))
    send(msend, mrecv, 13, dev_e(z_lo * 8 + ch))

    at = iota((64, 64), 0)
    source = bits(at, 2, 1) * 32 + bits(at, 5, 1) * 16 + bits(at, 3, 2) * 4 + bits(at, 0, 2)
    order = (source == iota((64, 64), 1)).astype(BF16)
    wasend[...] = nn(order, ab[...].reshape(64, 128)).astype(BF16)
    z6 = 4 * (1 - z_hi) + 2 * (1 - div(z_lo, 2)) + rem(z_lo, 2)

    def spread(src, dst, sem):
        each(0, 4, lambda k: send(src, dst, sem, place(rem(x + k, 4), z6)))
        each(1, 4, lambda k: send(src, dst, sem, place(rem(x + k, 4), z)))

    spread(wasend, warecv.at[ch], 1)
    wbsend[pl.ds(0, 16), :] = gate_weight[...]
    wbsend[pl.ds(16, 16), :] = out_weight[...]
    hsend[...] = jnp.zeros((8, 128), F32)
    hsend[pl.ds(0, 1), pl.ds(0, 16)] = hid_gain[...]
    hsend[pl.ds(1, 1), pl.ds(0, 16)] = hid_bias[...]
    spread(wbsend, wbrecv.at[ch], 2)
    spread(hsend, hrecv.at[ch], 3)
    warecv[ch] = wasend[...]
    wbrecv[ch] = wbsend[...]
    hrecv[ch] = hsend[...]

    eye = iota((128, 128), 0) == iota((128, 128), 1)
    gain_col = jnp.sum(jnp.where(eye, gain[...], 0.0), 1, keepdims=True)
    bias_col = jnp.sum(jnp.where(eye, bias[...], 0.0), 1, keepdims=True)

    wait_in(zrecv, 0)
    zn = norm(zrecv[...].astype(F32).reshape(128, RES), gain_col, bias_col).astype(BF16)
    wait_in(mrecv, 13)
    masking = jnp.concatenate([mrecv[pl.ds(kc, 1), :] for kc in range(4)], axis=1)
    wait_in(warecv.at[pl.ds(0, 7)], 1)
    opened = sigmoid(nn(warecv[:, pl.ds(0, 32), :].reshape(256, 128), zn))
    value = nn(warecv[:, pl.ds(32, 32), :].reshape(256, 128), zn)
    both = (opened * value * masking).reshape(32, 8, RES)
    lrsend[...] = jnp.concatenate([both[:, :, :256], both[:, :, 256:]], axis=1).astype(BF16)

    def other_e(k):
        return rem(e + k, 32)

    def other_b(k):
        return rem(b + k, 16)

    each(1, 32, lambda k: send(lrsend.at[other_e(k)], lrrecv.at[e], 4, dev_e(other_e(k))))
    lrrecv[e] = lrsend[e]

    wait_in(wbrecv.at[pl.ds(0, 7)], 2)
    gate = sigmoid(nn(wbrecv[:, pl.ds(0, 16), :].reshape(128, 128), zn)).T.reshape(8, 4, 2, 8, 128)
    for yy in range(8):
        for cc in range(2):
            gsend[yy * 2 + cc] = gate[yy, :, cc].reshape(32, 128).astype(BF16)
    each(1, 16, lambda k: send(gsend.at[other_b(k)], g1.at[b], 5, dev_b(other_b(k))))
    g1[b] = gsend[b]

    wait_in(lrrecv.at[pl.ds(0, 31)], 4)
    for lc in range(2):
        work[lc, :, :] = lrrecv[:, :, pl.ds(lc * 128, 128)].astype(F32).reshape(512, 128)
    for t in range(8):
        for kh in range(2):
            for lc in range(2):
                rows[t, :, pl.ds(kh * 256 + lc * 128, 128)] = work[lc, pl.ds(kh * 8 + t, 32, stride=16), :].astype(BF16)

    def share(k):
        h = rem(quarter + k, 4)
        send(rows.at[h], lbuf.at[quarter, core], 6, dev_b((half * 4 + h) * 2 + core))
        send(rows.at[4 + h], rbuf.at[y], 11, dev_b((half * 4 + h) * 2 + core))
        send(rows.at[4 + h], rbuf.at[y], 11, dev_b(((1 - half) * 4 + h) * 2 + core))

    each(1, 4, share)
    send(rows.at[4 + quarter], rbuf.at[y], 11, dev_b(((1 - half) * 4 + quarter) * 2 + core))
    lbuf[quarter, core] = rows[quarter]
    rbuf[y] = rows[4 + quarter]

    wait_in(g1.at[pl.ds(0, 15)], 5)
    work[2, :, :] = g1[...].astype(F32).reshape(512, 128)
    for j in range(32):
        g2send[j] = work[2, pl.ds(j, 16, stride=32), :].astype(BF16)
    each(1, 32, lambda k: send(g2send.at[other_e(k)], g2.at[e], 7, dev_e(other_e(k))))
    g2[e] = g2send[e]

    wait_in(rbuf.at[pl.ds(0, 3)], 6)
    send(lbuf.at[:, core], lbuf.at[:, core], 12, dev_b(y * 2 + 1 - core))

    def by_block(where, values):
        work[where, pl.ds(0, 128), :] = values
        return jnp.concatenate([work[where, pl.ds(h, 32, stride=4), :] for h in range(4)], axis=0)

    w_out = by_block(3, wbrecv[:, pl.ds(16, 16), :].astype(F32).reshape(128, 128))
    wout_t = nt(eye.astype(BF16), w_out.astype(BF16)).astype(BF16)
    wait_in(hrecv.at[pl.ds(0, 7)], 3)
    at_lane = iota((8, 16, 128), 1) == iota((8, 16, 128), 2)

    def column(row):
        col = jnp.sum(jnp.where(at_lane, hrecv[:, pl.ds(row, 1), :], 0.0), 2, keepdims=True)
        return by_block(3, jnp.broadcast_to(col, (8, 16, 128)).reshape(128, 128))

    hg, hb = column(0), column(1)
    lane = iota((128, 128), 0)
    natural = bits(lane, 6, 1) * 64 + bits(lane, 3, 2) * 16 + bits(lane, 5, 1) * 8 + bits(lane, 0, 3)
    perm = (natural == iota((128, 128), 1)).astype(BF16)

    wait_in(rbuf.at[pl.ds(0, 7)], 11)
    wait_in(rbuf.at[pl.ds(0, 4)], 12)
    tri = nt(rbuf[...].reshape(256, RES), lbuf[...].reshape(256, RES))
    tsend[...] = tri.astype(BF16).reshape(8, 32, 256)

    def back(k):
        y2 = rem(y + k, 8)
        send(tsend.at[y2], t1.at[y], 8, dev_b(y2 * 2 + core))

    each(1, 8, back)
    t1[y] = tsend[y]

    wait_in(g2.at[pl.ds(0, 31)], 7)
    work[2, :, :] = g2[...].astype(F32).reshape(512, 128)
    gate_t = jnp.concatenate([work[2, pl.ds(bb, 32, stride=16), :] for bb in range(16)], axis=0).T

    wait_in(t1.at[pl.ds(0, 7)], 8)
    for lc in range(2):
        work[lc, pl.ds(0, 256), :] = t1[:, :, pl.ds(lc * 128, 128)].astype(F32).reshape(256, 128)
    for j in range(32):
        t2send[j] = jnp.concatenate([work[lc, pl.ds(j, 8, stride=32), :] for lc in range(2)], axis=0).astype(BF16)
    each(1, 32, lambda k: send(t2send.at[other_e(k)], t2.at[e], 9, dev_e(other_e(k))))
    t2[e] = t2send[e]

    wait_in(t2.at[pl.ds(0, 31)], 9)
    work[0, :, :] = t2[...].astype(F32).reshape(512, 128)
    for tile in range(4):
        first = (tile % 2) * 8 + (tile // 2) * 4
        tri = jnp.concatenate([work[0, pl.ds(first + h, 32, stride=16), :] for h in range(4)], axis=0)
        tri_ln = norm(tri, hg, hb).astype(BF16)
        update = (nn(wout_t, tri_ln) * gate_t[:, tile * 128:tile * 128 + 128]).astype(BF16)
        usend[:, :, pl.ds(tile * 128, 128)] = nn(update, perm).astype(BF16).reshape(8, 16, 128)
    home = (y * 4 + e_lo) * 2 + core
    each(0, 8, lambda k: send(usend.at[rem(ch + k, 8)], out.at[e_ch], 10, (home, rem(ch + k, 8))))

    wait_out(zsend, 0)
    wait_out(warecv.at[pl.ds(0, 7)], 1)
    wait_out(wbrecv.at[pl.ds(0, 7)], 2)
    wait_out(hrecv.at[pl.ds(0, 7)], 3)
    wait_out(lrsend.at[pl.ds(0, 31)], 4)
    wait_out(gsend.at[pl.ds(0, 15)], 5)
    wait_out(rows.at[pl.ds(0, 3)], 6)
    wait_out(g2send.at[pl.ds(0, 31)], 7)
    wait_out(tsend.at[pl.ds(0, 7)], 8)
    wait_out(t2send.at[pl.ds(0, 31)], 9)
    wait_out(rows.at[pl.ds(0, 7)], 11)
    wait_out(rows.at[pl.ds(0, 4)], 12)
    wait_out(msend, 13)
    wait_out(usend, 10)
    wait_in(out, 10)


def body(pair, pair_mask, in_gain, in_bias, ab_weight, hid_gain, hid_bias, out_weight, gate_weight):
    vmem = pl.BlockSpec(memory_space=pltpu.VMEM)
    scratch = [
        ((4, 512, 128), F32),
        ((8, 16, RES), BF16), ((8, 16, RES), BF16),
        ((64, 128), BF16), ((8, 64, 128), BF16),
        ((32, 128), BF16), ((8, 32, 128), BF16),
        ((8, 128), F32), ((8, 8, 128), F32),
        ((8, 128), F32), ((8, 128), F32),
        ((32, 16, 256), BF16), ((32, 16, 256), BF16),
        ((8, 32, RES), BF16), ((4, 2, 32, RES), BF16), ((8, 32, RES), BF16),
        ((8, 32, 256), BF16), ((8, 32, 256), BF16),
        ((32, 16, 128), BF16), ((32, 16, 128), BF16),
        ((16, 32, 128), BF16), ((16, 32, 128), BF16),
        ((32, 16, 128), BF16), ((32, 16, 128), BF16),
        ((8, 16, RES), BF16),
    ]
    swapped = pl.pallas_call(
        kernel,
        out_shape=jax.ShapeDtypeStruct((8, 16, RES), BF16),
        in_specs=[vmem] * 9,
        out_specs=vmem,
        scratch_shapes=[pltpu.VMEM(shape, kind) for shape, kind in scratch]
        + [pltpu.SemaphoreType.DMA((14,)), pltpu.SemaphoreType.DMA((14,))],
        compiler_params=pltpu.CompilerParams(
            collective_id=0, has_side_effects=True, vmem_limit_bytes=32 * 1024 * 1024),
    )(pair, pair_mask, in_gain.reshape(1, CH), in_bias.reshape(1, CH), jnp.swapaxes(ab_weight, 1, 2),
      hid_gain.reshape(1, 16), hid_bias.reshape(1, 16), out_weight, gate_weight.T)
    return jnp.swapaxes(swapped, 0, 1)


def solution(mesh):
    placed = (
        P("ch", "dap", None),
        P("dap", None),
        P(),
        P(),
        P(None, None, "ch"),
        P("ch"),
        P("ch"),
        P("ch", None),
        P(None, "ch"),
    )
    return jax.shard_map(
        body, mesh=mesh, in_specs=placed, out_specs=P("ch", "dap", None), check_vma=False
    )
```

```python
import jax
import jax.numpy as jnp
from jax import lax
from jax.experimental import pallas as pl
from jax.experimental.pallas import tpu as pltpu
from jax.sharding import PartitionSpec as P

CH = 128
RES = 512
EPS = 1e-05
VMEM_LIMIT = 62 * 1024 * 1024
MESH = pl.DeviceIdType.MESH
F32 = jnp.float32
BF16 = jnp.bfloat16


def nt(a, b):
    return lax.dot_general(a, b, (((1,), (1,)), ((), ())), preferred_element_type=F32)


def nn(a, b):
    return lax.dot_general(a, b, (((1,), (0,)), ((), ())), preferred_element_type=F32)


def iota(shape, dim):
    return lax.broadcasted_iota(jnp.int32, shape, dim)


def bits(value, low, count):
    return lax.shift_right_logical(value, low) & ((1 << count) - 1)


def sigmoid(x):
    return 1.0 / (1.0 + jnp.exp(-x))


def norm(values, gain, bias):
    mean = jnp.sum(values, 0, keepdims=True) * (1.0 / CH)
    square = jnp.sum(values * values, 0, keepdims=True) * (1.0 / CH)
    var = square - mean * mean
    return (values - mean) * lax.rsqrt(var + EPS) * gain + bias


def each(first, last, body):
    def step(k, carry):
        body(k)
        return carry
    lax.fori_loop(first, last, step, 0)


def far(n, top):
    return top + lax.div(n + 1, 2) * (1 - 2 * lax.rem(n, 2))


def kernel(pair_in, mask_in, ab_in, gain_in, bias_in, gate_in, out_in, hid_gain_in, hid_bias_in, out,
           pair, mask, wasend, gain, bias, wbsend, hid_gain, hid_bias,
           work, zsend, zrecv, warecv, wbrecv, hsend, hrecv, msend, mrecv,
           rsend, rrecv, lsend, lrecv, rrows, lrows, lbuf, rbuf, tsend, t1, t2send, t2, gsend, g1, g2send, g2, usend,
           lsem, ssem, rsem):
    div, rem = lax.div, lax.rem
    dap = lax.axis_index("dap")
    ch = lax.axis_index("ch")
    x, z_hi = div(ch, 2), rem(ch, 2)
    y, z_lo, core = div(dap, 8), rem(div(dap, 2), 4), rem(dap, 2)
    z = z_hi * 4 + z_lo
    b = y * 2 + core
    e_lo, s = rem(z + 2, 4), div(rem(z + 6, 8), 4)
    e_ch = 2 * x + s
    u = rem(x, 2)
    f = e_lo * 4 + div(x, 2) * 2 + s
    e = u * 16 + f

    def place(x2, z2):
        return ((y * 4 + rem(z2, 4)) * 2 + core, x2 * 2 + div(z2, 4))

    def f_of(x2, z2):
        return rem(z2 + 2, 4) * 4 + div(x2, 2) * 2 + div(rem(z2 + 6, 8), 4)

    def dev_y(y2):
        return ((y2 * 4 + z_lo) * 2 + core, ch)

    sibling = (dap + 1 - 2 * core, ch)

    def send(src, dst, sem, device):
        pltpu.make_async_remote_copy(
            src_ref=src, dst_ref=dst, send_sem=ssem.at[sem], recv_sem=rsem.at[sem],
            device_id=device, device_id_type=MESH).start()

    def wait_in(ref, sem):
        pltpu.make_async_copy(ref, ref, rsem.at[sem]).wait()

    def wait_out(ref, sem):
        pltpu.make_async_copy(ref, ref, ssem.at[sem]).wait()

    def to_x(k):
        return rem(x + far(k, 2), 4)

    def to_y(k):
        return rem(y + far(k, 4), 8)

    def to_z(k):
        return rem(z + far(k, 4), 8)

    loads = [
        pltpu.make_async_copy(source, target, lsem.at[i]) for i, (source, target) in enumerate((
            (pair_in, pair), (mask_in, mask), (ab_in, wasend), (gate_in, wbsend.at[0]), (out_in, wbsend.at[1]),
            (gain_in, gain), (bias_in, bias), (hid_gain_in, hid_gain), (hid_bias_in, hid_bias)))
    ]
    for load in loads:
        load.start()

    barrier = pltpu.get_barrier_semaphore()

    def greet(device):
        pl.semaphore_signal(barrier, inc=1, device_id=device, device_id_type=MESH)

    def greet_y(k):
        y2 = to_y(div(k, 2))
        greet(((y2 * 4 + z_lo) * 2 + rem(core + 1 + k, 2), ch))

    each(0, 15, greet_y)
    each(0, 19, lambda k: greet(place(to_x(div(k, 5)), to_z(rem(k, 5) + 3))))

    for load in loads:
        load.wait()
    for kc in range(4):
        work[kc, pl.ds(0, 128), :] = pair[:, :, pl.ds(kc * 128, 128)].astype(F32).reshape(128, 128)
    for kc in range(4):
        for r in range(8):
            zsend[r, :, pl.ds(kc * 128, 128)] = work[kc, pl.ds(r, 16, stride=8), :].astype(BF16)
    own_mask = mask[pl.ds(ch, 1), :].astype(F32)
    for kc in range(4):
        msend[pl.ds(kc, 1), :] = own_mask[:, kc * 128:kc * 128 + 128]

    pl.semaphore_wait(barrier, 34)

    def first(k):
        x2, s2 = to_x(div(k, 2)), rem(s + k, 2)
        send(zsend.at[x2 * 2 + s2], zrecv.at[ch], 0, place(x2, rem(z_lo + 2 + 4 * s2, 8)))

    each(0, 8, first)
    send(msend, mrecv, 13, place(x, rem(z_lo + 2 + 4 * z_hi, 8)))

    z6 = 4 * (1 - z_hi) + 2 * (1 - div(z_lo, 2)) + rem(z_lo, 2)

    def spread(src, dst, sem):
        each(0, 4, lambda k: send(src, dst, sem, place(to_x(k), z6)))
        each(0, 3, lambda k: send(src, dst, sem, place(to_x(k), z)))

    spread(wasend.at[core], warecv.at[ch, core], 1)
    warecv[ch, core] = wasend[core]

    eye = iota((128, 128), 0) == iota((128, 128), 1)
    gain_col = jnp.sum(jnp.where(eye, gain[...], 0.0), 1, keepdims=True)
    bias_col = jnp.sum(jnp.where(eye, bias[...], 0.0), 1, keepdims=True)
    hsend[...] = jnp.zeros((1, 128), F32)
    hsend[:, pl.ds(0, 16)] = hid_gain[...]
    hsend[:, pl.ds(16, 16)] = hid_bias[...]

    wait_in(warecv.at[pl.ds(0, 7), 0], 1)
    send(warecv.at[:, core], warecv.at[:, core], 2, sibling)
    wait_in(zrecv, 0)
    zn = norm(zrecv[...].astype(F32).reshape(128, RES), gain_col, bias_col).astype(BF16)
    wait_in(mrecv, 13)
    masking = jnp.concatenate([mrecv[pl.ds(kc, 1), :] for kc in range(4)], axis=1)
    wait_in(warecv.at[:, 0], 2)

    def operand(side):
        weight = warecv[:, side]
        opened = sigmoid(nn(weight[:, :16].reshape(128, 128), zn))
        value = nn(weight[:, 16:].reshape(128, 128), zn)
        full = (opened * value * masking).reshape(16, 8, RES)
        return jnp.concatenate([full[:, :, :256], full[:, :, 256:]], axis=1).astype(BF16)

    def swap_f(sent, received, sem):
        def one(k):
            x2, z2 = rem(x + 2 * rem(k + 1, 2), 4), to_z(div(k, 2))
            send(sent.at[f_of(x2, z2)], received.at[f], sem, place(x2, z2))
        each(0, 15, one)
        received[f] = sent[f]

    rsend[...] = operand(1)
    swap_f(rsend, rrecv, 4)
    lsend[...] = operand(0)
    swap_f(lsend, lrecv, 14)
    spread(wbsend.at[core], wbrecv.at[ch, core], 3)
    spread(hsend, hrecv.at[ch], 16)
    wbrecv[ch, core] = wbsend[core]
    hrecv[ch] = hsend[...]

    def regroup(received, grouped, where):
        for lc in range(2):
            work[where + lc, pl.ds(0, 256), :] = received[:, :, pl.ds(lc * 128, 128)].astype(F32).reshape(256, 128)
        for h in range(8):
            for kh in range(2):
                for lc in range(2):
                    grouped[h, :, pl.ds(kh * 256 + lc * 128, 128)] = work[
                        where + lc, pl.ds(kh * 8 + h, 16, stride=16), :].astype(BF16)

    wait_in(rrecv.at[pl.ds(0, 15)], 4)
    regroup(rrecv, rrows, 0)
    each(0, 7, lambda k: send(rrows.at[to_y(k)], rbuf.at[y, u], 11, dev_y(to_y(k))))
    rbuf[y, u] = rrows[y]
    wait_in(lrecv.at[pl.ds(0, 15)], 14)
    regroup(lrecv, lrows, 2)
    each(0, 7, lambda k: send(lrows.at[to_y(k)], lbuf.at[y, core], 6, dev_y(to_y(k))))
    lbuf[y, core] = lrows[y]

    wait_in(wbrecv.at[pl.ds(0, 7), 0], 3)
    send(wbrecv.at[:, core], wbrecv.at[:, core], 17, sibling)
    wait_in(wbrecv.at[:, 0], 17)
    gate = sigmoid(nn(wbrecv[:, 0].reshape(128, 128), zn)).T.reshape(8, 4, 2, 8, 128)
    for yy in range(8):
        for cc in range(2):
            gsend[yy * 2 + cc] = gate[yy, :, cc].reshape(32, 128).astype(BF16)

    def gate_b(k):
        y2, core2 = to_y(div(k, 2)), rem(core + 1 + k, 2)
        send(gsend.at[y2 * 2 + core2], g1.at[b], 5, ((y2 * 4 + z_lo) * 2 + core2, ch))

    each(0, 15, gate_b)
    g1[b] = gsend[b]

    wait_in(rbuf.at[pl.ds(0, 7), 0], 11)
    send(rbuf.at[:, u], rbuf.at[:, u], 15, place(x + 1 - 2 * u, z))
    wait_in(lbuf.at[pl.ds(0, 7), 0], 6)
    send(lbuf.at[:, core], lbuf.at[:, core], 12, sibling)

    wait_in(g1.at[pl.ds(0, 15)], 5)
    work[2, :, :] = g1[...].astype(F32).reshape(512, 128)
    for j in range(32):
        lo, high, parity, low = j % 16 // 4, j % 4 // 2, j // 16, j % 2
        g2send[j] = work[2, pl.ds(lo * 8 + high * 4 + parity * 2 + low, 16, stride=32), :].astype(BF16)

    def gate_e(k):
        x2, z2 = to_x(rem(k, 4)), to_z(div(k, 4))
        send(g2send.at[rem(x2, 2) * 16 + f_of(x2, z2)], g2.at[e], 7, place(x2, z2))

    each(0, 31, gate_e)
    g2[e] = g2send[e]

    wout_t = nt(eye.astype(BF16), wbrecv[:, 1].reshape(128, 128)).astype(BF16)
    wait_in(hrecv.at[pl.ds(0, 7)], 16)
    at_gain = iota((8, 16, 128), 1) == iota((8, 16, 128), 2)
    at_bias = iota((8, 16, 128), 1) + 16 == iota((8, 16, 128), 2)

    def column(where):
        col = jnp.sum(jnp.where(where, hrecv[...], 0.0), 2, keepdims=True)
        return jnp.broadcast_to(col, (8, 16, 128)).reshape(128, 128)

    hg, hb = column(at_gain), column(at_bias)
    lane = iota((256, 256), 0)
    natural = (bits(lane, 5, 2) * 64 + bits(lane, 2, 2) * 16 + bits(lane, 4, 1) * 8
               + bits(lane, 1, 1) * 4 + bits(lane, 7, 1) * 2 + bits(lane, 0, 1))
    perm = (natural == iota((256, 256), 1)).astype(BF16)

    wait_in(lbuf.at[:, 0], 12)
    wait_in(rbuf.at[:, 0], 15)
    tri = nt(rbuf[...].reshape(256, RES), lbuf[...].reshape(256, RES))
    tsend[...] = tri.astype(BF16).reshape(8, 2, 16, 256)

    for part in range(2):
        v = u + part * (1 - 2 * u)
        each(0, 7, lambda k: send(tsend.at[to_y(k), v], t1.at[part, y], 8 + part, dev_y(to_y(k))))
        t1[part, y] = tsend[y, v]

    wait_in(g2.at[pl.ds(0, 31)], 7)
    work[2, :, :] = g2[...].astype(F32).reshape(512, 128)
    gate_t = jnp.concatenate(
        [work[2, pl.ds(uu * 256 + bb, 16, stride=16), :] for uu in range(2) for bb in range(16)], axis=0).T

    for part in range(2):
        wait_in(t1.at[part, pl.ds(0, 7)], 8 + part)
        for lc in range(2):
            work[lc, pl.ds(0, 128), :] = t1[part, :, :, pl.ds(lc * 128, 128)].astype(F32).reshape(128, 128)
        for j in range(16):
            t2send[part * 16 + j] = jnp.concatenate(
                [work[lc, pl.ds(j, 8, stride=16), :] for lc in range(2)], axis=0).astype(BF16)

        def forward(k):
            x2, z2 = rem(x + (2 * rem(k + 1, 2) if part == 0 else 1 + 2 * rem(k, 2)), 4), to_z(div(k, 2))
            send(t2send.at[part * 16 + f_of(x2, z2)], t2.at[e], 10, place(x2, z2))

        each(0, 16 - (part == 0), forward)
    t2[e] = t2send[f]

    wait_in(t2.at[pl.ds(0, 31)], 10)
    tiles = t2[...].astype(F32).reshape(2, 16, 2, 8, 128)
    for lt in range(2):
        parts = []
        for uu in range(2):
            tri_ln = norm(tiles[uu, :, lt].reshape(128, 128), hg, hb).astype(BF16)
            at = uu * 256 + lt * 128
            parts.append((nn(wout_t, tri_ln) * gate_t[:, at:at + 128]).astype(BF16))
        update = nn(jnp.concatenate(parts, axis=1), perm)
        usend[:, :, pl.ds(lt * 256, 256)] = update.astype(BF16).reshape(8, 16, 256)

    def last(k):
        x2, half = to_x(div(k, 2)), rem(z_hi + k, 2)
        send(usend.at[x2 * 2 + half], out.at[e_ch], 18, place(x2, e_lo + 4 * half))

    each(0, 8, last)

    wait_out(zsend, 0)
    wait_out(warecv.at[pl.ds(0, 7), 0], 1)
    wait_out(warecv.at[:, 0], 2)
    wait_out(wbrecv.at[pl.ds(0, 7), 0], 3)
    wait_out(rsend.at[pl.ds(0, 15)], 4)
    wait_out(gsend.at[pl.ds(0, 15)], 5)
    wait_out(lrows.at[pl.ds(0, 7)], 6)
    wait_out(g2send.at[pl.ds(0, 31)], 7)
    wait_out(t1.at[0, pl.ds(0, 7)], 8)
    wait_out(t1.at[1, pl.ds(0, 7)], 9)
    wait_out(t2send.at[pl.ds(0, 31)], 10)
    wait_out(rrows.at[pl.ds(0, 7)], 11)
    wait_out(lbuf.at[:, 0], 12)
    wait_out(msend, 13)
    wait_out(lsend.at[pl.ds(0, 15)], 14)
    wait_out(rbuf.at[:, 0], 15)
    wait_out(hrecv.at[pl.ds(0, 7)], 16)
    wait_out(wbrecv.at[:, 0], 17)
    wait_out(usend, 18)
    wait_in(out, 18)


def body(pair, pair_mask, in_gain, in_bias, ab_weight, hid_gain, hid_bias, out_weight, gate_weight):
    rows = pair.shape[1]
    scratch = [
        ((16, rows, RES), BF16), ((rows, RES), jnp.int32), ((2, 32, 128), BF16),
        ((1, CH), F32), ((1, CH), F32), ((2, 16, 128), BF16), ((1, 16), F32), ((1, 16), F32),
        ((4, 512, 128), F32),
        ((8, 16, RES), BF16), ((8, 16, RES), BF16),
        ((8, 2, 32, 128), BF16), ((8, 2, 16, 128), BF16),
        ((1, 128), F32), ((8, 1, 128), F32),
        ((8, 128), F32), ((8, 128), F32),
        ((16, 16, 256), BF16), ((16, 16, 256), BF16), ((16, 16, 256), BF16), ((16, 16, 256), BF16),
        ((8, 16, RES), BF16), ((8, 16, RES), BF16), ((8, 2, 16, RES), BF16), ((8, 2, 16, RES), BF16),
        ((8, 2, 16, 256), BF16), ((2, 8, 16, 256), BF16),
        ((32, 16, 128), BF16), ((32, 16, 128), BF16),
        ((16, 32, 128), BF16), ((16, 32, 128), BF16),
        ((32, 16, 128), BF16), ((32, 16, 128), BF16),
        ((8, 16, RES), BF16),
    ]
    swapped = pl.pallas_call(
        kernel,
        out_shape=jax.ShapeDtypeStruct((8, 16, RES), BF16),
        in_specs=[pl.BlockSpec(memory_space=pltpu.HBM)] * 9,
        out_specs=pl.BlockSpec(memory_space=pltpu.VMEM),
        scratch_shapes=[pltpu.VMEM(shape, kind) for shape, kind in scratch]
        + [pltpu.SemaphoreType.DMA((9,)), pltpu.SemaphoreType.DMA((19,)), pltpu.SemaphoreType.DMA((19,))],
        compiler_params=pltpu.CompilerParams(
            collective_id=0, has_side_effects=True, vmem_limit_bytes=VMEM_LIMIT),
    )(pair, pair_mask, jnp.swapaxes(ab_weight, 1, 2).reshape(2, 32, CH), in_gain.reshape(1, CH), in_bias.reshape(1, CH),
      gate_weight.T, out_weight, hid_gain.reshape(1, 16), hid_bias.reshape(1, 16))
    return jnp.swapaxes(swapped, 0, 1)


def solution(mesh):
    placed = (
        P("ch", "dap", None),
        P("dap", None),
        P(),
        P(),
        P(None, None, "ch"),
        P("ch"),
        P("ch"),
        P("ch", None),
        P(None, "ch"),
    )
    return jax.shard_map(
        body, mesh=mesh, in_specs=placed, out_specs=P("ch", "dap", None), check_vma=False
    )
```

```python
import jax
import jax.numpy as jnp
from jax import lax
from jax.experimental import pallas as pl
from jax.experimental.pallas import tpu as pltpu
from jax.sharding import PartitionSpec as P

CH = 128
RES = 512
EPS = 1e-05
VMEM_LIMIT = 62 * 1024 * 1024
MESH = pl.DeviceIdType.MESH
F32 = jnp.float32
BF16 = jnp.bfloat16


def nt(a, b):
    return lax.dot_general(a, b, (((1,), (1,)), ((), ())), preferred_element_type=F32)


def nn(a, b):
    return lax.dot_general(a, b, (((1,), (0,)), ((), ())), preferred_element_type=F32)


def iota(shape, dim):
    return lax.broadcasted_iota(jnp.int32, shape, dim)


def bits(value, low, count):
    return lax.shift_right_logical(value, low) & ((1 << count) - 1)


def sigmoid(x):
    return 1.0 / (1.0 + jnp.exp(-x))


def norm(values, gain, bias):
    mean = jnp.sum(values, 0, keepdims=True) * (1.0 / CH)
    square = jnp.sum(values * values, 0, keepdims=True) * (1.0 / CH)
    var = square - mean * mean
    return (values - mean) * lax.rsqrt(var + EPS) * gain + bias


def each(first, last, body):
    def step(k, carry):
        body(k)
        return carry
    lax.fori_loop(first, last, step, 0, unroll=True)


def far(n, top):
    return top + lax.div(n + 1, 2) * (1 - 2 * lax.rem(n, 2))


def kernel(pair_in, mask_in, ab_in, gain_in, bias_in, gate_in, out_in, hid_gain_in, hid_bias_in, out,
           pair, mask, wsend, gain, bias, hid_gain, hid_bias,
           work, zsend, zrecv, wrecv, hsend, hrecv, msend, mrecv,
           rsend, rrecv, rrows, rbuf, lsend, lmid, lrows, lrecv, lbuf, tsend, t1, t2send, t2, gsend, g1, g2send, g2, usend,
           lsem, ssem, rsem):
    div, rem = lax.div, lax.rem
    dap = lax.axis_index("dap")
    ch = lax.axis_index("ch")
    x, z_hi = div(ch, 2), rem(ch, 2)
    y, z_lo, core = div(dap, 8), rem(div(dap, 2), 4), rem(dap, 2)
    z = z_hi * 4 + z_lo
    b = y * 2 + core
    e_lo, s = rem(z + 2, 4), div(rem(z + 6, 8), 4)
    e_ch = 2 * x + s
    u = rem(x, 2)
    f = e_lo * 4 + div(x, 2) * 2 + s
    e = u * 16 + f

    def place(x2, z2):
        return ((y * 4 + rem(z2, 4)) * 2 + core, x2 * 2 + div(z2, 4))

    def f_of(x2, z2):
        return rem(z2 + 2, 4) * 4 + div(x2, 2) * 2 + div(rem(z2 + 6, 8), 4)

    def dev_y(y2):
        return ((y2 * 4 + z_lo) * 2 + core, ch)

    sibling = (dap + 1 - 2 * core, ch)

    def send(src, dst, sem, device):
        pltpu.make_async_remote_copy(
            src_ref=src, dst_ref=dst, send_sem=ssem.at[sem], recv_sem=rsem.at[sem],
            device_id=device, device_id_type=MESH).start()

    def wait_in(ref, sem):
        pltpu.make_async_copy(ref, ref, rsem.at[sem]).wait()

    def wait_out(ref, sem):
        pltpu.make_async_copy(ref, ref, ssem.at[sem]).wait()

    def to_x(k):
        return rem(x + far(k, 2), 4)

    def to_y(k):
        return rem(y + far(k, 4), 8)

    def to_z(k):
        return rem(z + far(k, 4), 8)

    loads = [
        pltpu.make_async_copy(source, target, lsem.at[i]) for i, (source, target) in enumerate((
            (pair_in, pair), (mask_in, mask), (ab_in, wsend.at[:, pl.ds(0, 32)]),
            (gate_in, wsend.at[0, pl.ds(32, 16)]), (out_in, wsend.at[1, pl.ds(32, 16)]),
            (gain_in, gain), (bias_in, bias), (hid_gain_in, hid_gain), (hid_bias_in, hid_bias)))
    ]
    for load in loads:
        load.start()

    barrier = pltpu.get_barrier_semaphore()

    def greet(device):
        pl.semaphore_signal(barrier, inc=1, device_id=device, device_id_type=MESH)

    def greet_y(k):
        y2 = to_y(div(k, 2))
        greet(((y2 * 4 + z_lo) * 2 + rem(core + 1 + k, 2), ch))

    each(0, 15, greet_y)
    each(0, 19, lambda k: greet(place(to_x(div(k, 5)), to_z(rem(k, 5) + 3))))

    for load in loads:
        load.wait()
    for kc in range(4):
        work[kc, pl.ds(0, 128), :] = pair[:, :, pl.ds(kc * 128, 128)].astype(F32).reshape(128, 128)
    for kc in range(4):
        for r in range(8):
            zsend[r, :, pl.ds(kc * 128, 128)] = work[kc, pl.ds(r, 16, stride=8), :].astype(BF16)
    own_mask = mask[pl.ds(ch, 1), :].astype(F32)
    for kc in range(4):
        msend[pl.ds(kc, 1), :] = own_mask[:, kc * 128:kc * 128 + 128]

    pl.semaphore_wait(barrier, 34)

    def first(k):
        x2, s2 = to_x(div(k, 2)), rem(s + k, 2)
        send(zsend.at[x2 * 2 + s2], zrecv.at[ch], 0, place(x2, rem(z_lo + 2 + 4 * s2, 8)))

    z6 = 4 * (1 - z_hi) + 2 * (1 - div(z_lo, 2)) + rem(z_lo, 2)
    crossed = x * 2 + 1 - z_hi

    def along_x(src, dst, sem):
        each(0, 3, lambda k: send(src, dst, sem, place(to_x(k), z)))

    send(wsend.at[core], wrecv.at[ch, core], 1, place(x, z6))
    each(0, 8, first)
    send(msend, mrecv, 13, place(x, rem(z_lo + 2 + 4 * z_hi, 8)))
    along_x(wsend.at[core], wrecv.at[ch, core], 2)
    wrecv[ch, core] = wsend[core]

    eye = iota((128, 128), 0) == iota((128, 128), 1)
    gain_col = jnp.sum(jnp.where(eye, gain[...], 0.0), 1, keepdims=True)
    bias_col = jnp.sum(jnp.where(eye, bias[...], 0.0), 1, keepdims=True)
    hsend[...] = jnp.zeros((1, 128), F32)
    hsend[:, pl.ds(0, 16)] = hid_gain[...]
    hsend[:, pl.ds(16, 16)] = hid_bias[...]

    wait_in(wrecv.at[0, 0], 1)
    along_x(wrecv.at[crossed, core], wrecv.at[crossed, core], 3)
    wait_in(zrecv, 0)
    wait_in(wrecv.at[pl.ds(0, 3), 0], 2)
    wait_in(wrecv.at[pl.ds(0, 3), 0], 3)
    send(wrecv.at[:, core], wrecv.at[:, core], 17, sibling)
    zn = norm(zrecv[...].astype(F32).reshape(128, RES), gain_col, bias_col).astype(BF16)
    wait_in(mrecv, 13)
    masking = jnp.concatenate([mrecv[pl.ds(kc, 1), :] for kc in range(4)], axis=1)
    wait_in(wrecv.at[:, 0], 17)

    def operand(side):
        opened = sigmoid(nn(wrecv[:, side, pl.ds(0, 16)].reshape(128, 128), zn))
        value = nn(wrecv[:, side, pl.ds(16, 16)].reshape(128, 128), zn)
        return opened * value * masking

    def swap_f(sent, received, sem):
        def one(k):
            x2, z2 = rem(x + 2 * rem(k + 1, 2), 4), to_z(div(k, 2))
            send(sent.at[f_of(x2, z2)], received.at[f], sem, place(x2, z2))
        each(0, 15, one)
        received[f] = sent[f]

    def swap_y(sent, slot, sem):
        each(0, 7, lambda k: send(sent.at[to_y(k)], slot, sem, dev_y(to_y(k))))

    right = operand(1).reshape(16, 8, RES)
    for kh in range(2):
        at = kh * 256
        rsend[kh] = jnp.concatenate([right[:, :, at:at + 128], right[:, :, at + 128:at + 256]], axis=1).astype(BF16)
        swap_f(rsend.at[kh], rrecv.at[kh], 4 + 15 * kh)
    left = operand(0)
    for lc in range(4):
        work[lc, pl.ds(0, 128), :] = left[:, lc * 128:lc * 128 + 128]
    for lc in range(4):
        for h in range(8):
            lsend[h, :, pl.ds(lc * 128, 128)] = work[lc, pl.ds(h, 16, stride=8), :].astype(BF16)
    swap_y(lsend, lmid.at[y], 14)
    lmid[y] = lsend[y]
    each(0, 4, lambda k: send(hsend, hrecv.at[ch], 16, place(to_x(k), z6)))
    along_x(hsend, hrecv.at[ch], 16)
    hrecv[ch] = hsend[...]

    gate = sigmoid(nn(wrecv[:, 0, pl.ds(32, 16)].reshape(128, 128), zn)).T.reshape(8, 4, 2, 8, 128)
    for yy in range(8):
        for cc in range(2):
            gsend[yy * 2 + cc] = gate[yy, :, cc].reshape(32, 128).astype(BF16)

    def gate_b(k):
        y2, core2 = to_y(div(k, 2)), rem(core + 1 + k, 2)
        send(gsend.at[y2 * 2 + core2], g1.at[b], 5, ((y2 * 4 + z_lo) * 2 + core2, ch))

    each(0, 15, gate_b)
    g1[b] = gsend[b]

    def spread_right(kh):
        wait_in(rrecv.at[kh, pl.ds(0, 15)], 4 + 15 * kh)
        work[kh, pl.ds(0, 256), :] = rrecv[kh].astype(F32).reshape(256, 128)
        for h in range(8):
            for lc in range(2):
                rrows[kh, h, :, pl.ds(lc * 128, 128)] = work[kh, pl.ds(lc * 8 + h, 16, stride=16), :].astype(BF16)
        swap_y(rrows.at[kh], rbuf.at[kh, y, u], 11 + 9 * kh)
        rbuf[kh, y, u] = rrows[kh, y]

    spread_right(0)
    wait_in(lmid.at[pl.ds(0, 7)], 14)
    for lc in range(4):
        work[lc, pl.ds(256, 128), :] = lmid[:, :, pl.ds(lc * 128, 128)].astype(F32).reshape(128, 128)
    for g in range(16):
        for lc in range(2):
            lrows[g, :, pl.ds(lc * 128, 128)] = jnp.concatenate(
                [work[kh * 2 + lc, pl.ds(256 + g, 8, stride=16), :] for kh in range(2)], axis=0).astype(BF16)
    swap_f(lrows, lrecv, 6)
    spread_right(1)

    for kh in range(2):
        wait_in(rbuf.at[0, pl.ds(0, 7), 0], 11 + 9 * kh)
        send(rbuf.at[kh, :, u], rbuf.at[kh, :, u], 15 + 6 * kh, place(x + 1 - 2 * u, z))

    wout_t = nt(eye.astype(BF16), wrecv[:, 1, pl.ds(32, 16)].reshape(128, 128)).astype(BF16)
    wait_in(hrecv.at[pl.ds(0, 7)], 16)
    at_gain = iota((8, 16, 128), 1) == iota((8, 16, 128), 2)
    at_bias = iota((8, 16, 128), 1) + 16 == iota((8, 16, 128), 2)

    def column(where):
        col = jnp.sum(jnp.where(where, hrecv[...], 0.0), 2, keepdims=True)
        return jnp.broadcast_to(col, (8, 16, 128)).reshape(128, 128)

    hg, hb = column(at_gain), column(at_bias)
    lane = iota((256, 256), 0)
    natural = (bits(lane, 5, 2) * 64 + bits(lane, 2, 2) * 16 + bits(lane, 4, 1) * 8
               + bits(lane, 1, 1) * 4 + bits(lane, 7, 1) * 2 + bits(lane, 0, 1))
    perm = (natural == iota((256, 256), 1)).astype(BF16)

    wait_in(lrecv.at[pl.ds(0, 15)], 6)
    for lc in range(2):
        work[2 + lc, pl.ds(0, 256), :] = lrecv[:, :, pl.ds(lc * 128, 128)].astype(F32).reshape(256, 128)
    for kh in range(2):
        for yy in range(8):
            for lc in range(2):
                lbuf[kh, yy, core, :, pl.ds(lc * 128, 128)] = work[2 + lc, pl.ds(kh * 8 + yy, 16, stride=16), :].astype(BF16)
    send(lbuf.at[:, :, core], lbuf.at[:, :, core], 12, sibling)
    wait_in(rbuf.at[0, :, 0], 15)
    wait_in(rbuf.at[1, :, 0], 21)
    wait_in(lbuf.at[:, :, 0], 12)
    tri = nt(rbuf[0].reshape(256, 256), lbuf[0].reshape(256, 256)) + nt(rbuf[1].reshape(256, 256), lbuf[1].reshape(256, 256))
    tsend[...] = tri.astype(BF16).reshape(8, 2, 16, 256)

    for v in range(2):
        each(0, 7, lambda k: send(tsend.at[to_y(k), v], t1.at[v, y], 8 + v, dev_y(to_y(k))))
        t1[v, y] = tsend[y, v]

    wait_in(g1.at[pl.ds(0, 15)], 5)
    work[2, :, :] = g1[...].astype(F32).reshape(512, 128)
    for j in range(32):
        lo, high, parity, low = j % 16 // 4, j % 4 // 2, j // 16, j % 2
        g2send[j] = work[2, pl.ds(lo * 8 + high * 4 + parity * 2 + low, 16, stride=32), :].astype(BF16)

    def gate_e(k):
        x2, z2 = to_x(rem(k, 4)), to_z(div(k, 4))
        send(g2send.at[rem(x2, 2) * 16 + f_of(x2, z2)], g2.at[e], 7, place(x2, z2))

    each(0, 31, gate_e)
    g2[e] = g2send[e]

    for v in range(2):
        wait_in(t1.at[v, pl.ds(0, 7)], 8 + v)
        for lc in range(2):
            work[lc, pl.ds(0, 128), :] = t1[v, :, :, pl.ds(lc * 128, 128)].astype(F32).reshape(128, 128)
        for j in range(16):
            t2send[v * 16 + j] = jnp.concatenate(
                [work[lc, pl.ds(j, 8, stride=16), :] for lc in range(2)], axis=0).astype(BF16)
        w = rem(u + v, 2)

        def forward(k):
            x2, z2 = rem(x + 2 - w + rem(k, 2) * (4 * w - 2), 4), to_z(div(k, 2))
            send(t2send.at[v * 16 + f_of(x2, z2)], t2.at[e], 10, place(x2, z2))

        each(0, 15, forward)

        @pl.when(w == 1)
        def _():
            forward(15)

        @pl.when(w == 0)
        def _():
            t2[e] = t2send[v * 16 + f]

    wait_in(g2.at[pl.ds(0, 31)], 7)
    work[2, :, :] = g2[...].astype(F32).reshape(512, 128)
    gate_t = jnp.concatenate(
        [work[2, pl.ds(uu * 256 + bb, 16, stride=16), :] for uu in range(2) for bb in range(16)], axis=0).T

    wait_in(t2.at[pl.ds(0, 31)], 10)
    tiles = t2[...].astype(F32).reshape(2, 16, 2, 8, 128)
    for lt in range(2):
        parts = []
        for uu in range(2):
            tri_ln = norm(tiles[uu, :, lt].reshape(128, 128), hg, hb).astype(BF16)
            at = uu * 256 + lt * 128
            parts.append((nn(wout_t, tri_ln) * gate_t[:, at:at + 128]).astype(BF16))
        update = nn(jnp.concatenate(parts, axis=1), perm)
        usend[lt] = update.astype(BF16).reshape(8, 16, 256)

        def last(k):
            x2, half = to_x(div(k, 2)), rem(z_hi + k, 2)
            send(usend.at[lt, x2 * 2 + half], out.at[e_ch, :, pl.ds(lt * 256, 256)], 18, place(x2, e_lo + 4 * half))

        each(0, 8, last)

    wait_out(zsend, 0)
    wait_out(wsend.at[0], 1)
    wait_out(wrecv.at[pl.ds(0, 3), 0], 2)
    wait_out(wrecv.at[pl.ds(0, 3), 0], 3)
    wait_out(rsend.at[0, pl.ds(0, 15)], 4)
    wait_out(rsend.at[1, pl.ds(0, 15)], 19)
    wait_out(lsend.at[pl.ds(0, 7)], 14)
    wait_out(gsend.at[pl.ds(0, 15)], 5)
    wait_out(lrows.at[pl.ds(0, 15)], 6)
    wait_out(g2send.at[pl.ds(0, 31)], 7)
    wait_out(t1.at[0, pl.ds(0, 7)], 8)
    wait_out(t1.at[1, pl.ds(0, 7)], 9)
    wait_out(t2send.at[pl.ds(0, 31)], 10)
    wait_out(rrows.at[0, pl.ds(0, 7)], 11)
    wait_out(rrows.at[1, pl.ds(0, 7)], 20)
    wait_out(lbuf.at[:, :, 0], 12)
    wait_out(msend, 13)
    wait_out(rbuf.at[0, :, 0], 15)
    wait_out(rbuf.at[1, :, 0], 21)
    wait_out(hrecv.at[pl.ds(0, 7)], 16)
    wait_out(wrecv.at[:, 0], 17)
    wait_out(usend, 18)
    wait_in(out, 18)


def body(pair, pair_mask, in_gain, in_bias, ab_weight, hid_gain, hid_bias, out_weight, gate_weight):
    rows = pair.shape[1]
    scratch = [
        ((16, rows, RES), BF16), ((rows, RES), jnp.int32), ((2, 48, 128), BF16),
        ((1, CH), F32), ((1, CH), F32), ((1, 16), F32), ((1, 16), F32),
        ((4, 512, 128), F32),
        ((8, 16, RES), BF16), ((8, 16, RES), BF16),
        ((8, 2, 48, 128), BF16),
        ((1, 128), F32), ((8, 1, 128), F32),
        ((8, 128), F32), ((8, 128), F32),
        ((2, 16, 16, 128), BF16), ((2, 16, 16, 128), BF16), ((2, 8, 16, 256), BF16), ((2, 8, 2, 16, 256), BF16),
        ((8, 16, RES), BF16), ((8, 16, RES), BF16), ((16, 16, 256), BF16), ((16, 16, 256), BF16), ((2, 8, 2, 16, 256), BF16),
        ((8, 2, 16, 256), BF16), ((2, 8, 16, 256), BF16),
        ((32, 16, 128), BF16), ((32, 16, 128), BF16),
        ((16, 32, 128), BF16), ((16, 32, 128), BF16),
        ((32, 16, 128), BF16), ((32, 16, 128), BF16),
        ((2, 8, 16, 256), BF16),
    ]
    swapped = pl.pallas_call(
        kernel,
        out_shape=jax.ShapeDtypeStruct((8, 16, RES), BF16),
        in_specs=[pl.BlockSpec(memory_space=pltpu.HBM)] * 9,
        out_specs=pl.BlockSpec(memory_space=pltpu.VMEM),
        scratch_shapes=[pltpu.VMEM(shape, kind) for shape, kind in scratch]
        + [pltpu.SemaphoreType.DMA((9,)), pltpu.SemaphoreType.DMA((22,)), pltpu.SemaphoreType.DMA((22,))],
        compiler_params=pltpu.CompilerParams(
            collective_id=0, has_side_effects=True, vmem_limit_bytes=VMEM_LIMIT),
    )(pair, pair_mask, jnp.swapaxes(ab_weight, 1, 2).reshape(2, 32, CH), in_gain.reshape(1, CH), in_bias.reshape(1, CH),
      gate_weight.T, out_weight, hid_gain.reshape(1, 16), hid_bias.reshape(1, 16))
    return jnp.swapaxes(swapped, 0, 1)


def solution(mesh):
    placed = (
        P("ch", "dap", None),
        P("dap", None),
        P(),
        P(),
        P(None, None, "ch"),
        P("ch"),
        P("ch"),
        P("ch", None),
        P(None, "ch"),
    )
    return jax.shard_map(
        body, mesh=mesh, in_specs=placed, out_specs=P("ch", "dap", None), check_vma=False
    )
```

```python
import jax
import jax.numpy as jnp
from jax import lax
from jax.experimental import pallas as pl
from jax.experimental.pallas import tpu as pltpu
from jax.sharding import PartitionSpec as P

CH = 128
RES = 512
EPS = 1e-05
VMEM_LIMIT = 62 * 1024 * 1024
MESH = pl.DeviceIdType.MESH
F32 = jnp.float32
BF16 = jnp.bfloat16


def nt(a, b):
    return lax.dot_general(a, b, (((1,), (1,)), ((), ())), preferred_element_type=F32)


def nn(a, b):
    return lax.dot_general(a, b, (((1,), (0,)), ((), ())), preferred_element_type=F32)


def iota(shape, dim):
    return lax.broadcasted_iota(jnp.int32, shape, dim)


def bits(value, low, count):
    return lax.shift_right_logical(value, low) & ((1 << count) - 1)


def sigmoid(x):
    return 1.0 / (1.0 + jnp.exp(-x))


def norm(values, gain, bias):
    mean = jnp.sum(values, 0, keepdims=True) * (1.0 / CH)
    square = jnp.sum(values * values, 0, keepdims=True) * (1.0 / CH)
    var = square - mean * mean
    return (values - mean) * lax.rsqrt(var + EPS) * gain + bias


def each(first, last, body):
    def step(k, carry):
        body(k)
        return carry
    lax.fori_loop(first, last, step, 0, unroll=True)


def far(n, top):
    return top + lax.div(n + 1, 2) * (1 - 2 * lax.rem(n, 2))


def kernel(pair_in, mask_in, ab_in, gain_in, bias_in, gate_in, out_in, hid_gain_in, hid_bias_in, out,
           pair, mask, wsend, gain, bias, hid_gain, hid_bias,
           work, zsend, zrecv, wrecv, hsend, hrecv, msend, mrecv,
           rsend, rrecv, rrows, rbuf, lsend, lmid, lrows, lrecv, lbuf, tsend, t1, t2send, t2, gsend, g1, g2send, g2, usend,
           lsem, ssem, rsem):
    div, rem = lax.div, lax.rem
    dap = lax.axis_index("dap")
    ch = lax.axis_index("ch")
    x, z_hi = div(ch, 2), rem(ch, 2)
    y, z_lo, core = div(dap, 8), rem(div(dap, 2), 4), rem(dap, 2)
    z = z_hi * 4 + z_lo
    b = y * 2 + core
    e_lo, s = rem(z + 2, 4), div(rem(z + 6, 8), 4)
    e_ch = 2 * x + s
    u = rem(x, 2)
    f = e_lo * 4 + div(x, 2) * 2 + s
    e = u * 16 + f

    def place(x2, z2):
        return ((y * 4 + rem(z2, 4)) * 2 + core, x2 * 2 + div(z2, 4))

    def f_of(x2, z2):
        return rem(z2 + 2, 4) * 4 + div(x2, 2) * 2 + div(rem(z2 + 6, 8), 4)

    def dev_y(y2):
        return ((y2 * 4 + z_lo) * 2 + core, ch)

    sibling = (dap + 1 - 2 * core, ch)

    def send(src, dst, sem, device):
        pltpu.make_async_remote_copy(
            src_ref=src, dst_ref=dst, send_sem=ssem.at[sem], recv_sem=rsem.at[sem],
            device_id=device, device_id_type=MESH).start()

    def wait_in(ref, sem):
        pltpu.make_async_copy(ref, ref, rsem.at[sem]).wait()

    def wait_out(ref, sem):
        pltpu.make_async_copy(ref, ref, ssem.at[sem]).wait()

    def to_x(k):
        return rem(x + far(k, 2), 4)

    def to_y(k):
        return rem(y + far(k, 4), 8)

    def to_z(k):
        return rem(z + far(k, 4), 8)

    loads = [
        pltpu.make_async_copy(source, target, lsem.at[i]) for i, (source, target) in enumerate((
            (pair_in, pair), (mask_in, mask), (ab_in, wsend.at[:, pl.ds(0, 32)]),
            (gate_in, wsend.at[0, pl.ds(32, 16)]), (out_in, wsend.at[1, pl.ds(32, 16)]),
            (gain_in, gain), (bias_in, bias), (hid_gain_in, hid_gain), (hid_bias_in, hid_bias)))
    ]
    for load in loads:
        load.start()

    barrier = pltpu.get_barrier_semaphore()

    def greet(device):
        pl.semaphore_signal(barrier, inc=1, device_id=device, device_id_type=MESH)

    greet(dev_y(rem(y + 4, 8)))
    each(0, 8, lambda k: greet(place(to_x(div(k, 2)), rem(z + 2 + 4 * rem(k, 2), 8))))
    each(1, 7, lambda k: greet(dev_y(to_y(k))))
    each(0, 3, lambda k: greet(place(to_x(k), z)))
    each(0, 2, lambda k: greet(place(x, rem(z + 1 + 6 * k, 8))))
    greet(sibling)

    for load in loads:
        load.wait()
    for kc in range(4):
        work[kc, pl.ds(0, 128), :] = pair[:, :, pl.ds(kc * 128, 128)].astype(F32).reshape(128, 128)
    for kc in range(4):
        for r in range(8):
            zsend[r, :, pl.ds(kc * 128, 128)] = work[kc, pl.ds(r, 16, stride=8), :].astype(BF16)
    own_mask = mask[pl.ds(ch, 1), :].astype(F32)
    for kc in range(4):
        msend[pl.ds(kc, 1), :] = own_mask[:, kc * 128:kc * 128 + 128]

    pl.semaphore_wait(barrier, 21)

    def first(k):
        x2, s2 = to_x(div(k, 2)), rem(s + k, 2)
        send(zsend.at[x2 * 2 + s2], zrecv.at[ch], 0, place(x2, rem(z_lo + 2 + 4 * s2, 8)))

    z6 = 4 * (1 - z_hi) + 2 * (1 - div(z_lo, 2)) + rem(z_lo, 2)
    crossed = x * 2 + 1 - z_hi

    def along_x(src, dst, sem):
        each(0, 3, lambda k: send(src, dst, sem, place(to_x(k), z)))

    each(0, 4, lambda k: send(wsend.at[core, pl.ds(0, 32)], wrecv.at[ch, core, pl.ds(0, 32)], 2, place(to_x(k), z6)))
    along_x(wsend.at[core, pl.ds(0, 32)], wrecv.at[ch, core, pl.ds(0, 32)], 2)
    each(0, 8, first)
    each(0, 4, lambda k: send(wsend.at[core, pl.ds(32, 16)], wrecv.at[ch, core, pl.ds(32, 16)], 3, place(to_x(k), z6)))
    along_x(wsend.at[core, pl.ds(32, 16)], wrecv.at[ch, core, pl.ds(32, 16)], 3)
    send(msend, mrecv, 13, place(x, rem(z_lo + 2 + 4 * z_hi, 8)))
    wrecv[ch, core] = wsend[core]

    eye = iota((128, 128), 0) == iota((128, 128), 1)
    gain_col = jnp.sum(jnp.where(eye, gain[...], 0.0), 1, keepdims=True)
    bias_col = jnp.sum(jnp.where(eye, bias[...], 0.0), 1, keepdims=True)
    hsend[...] = jnp.zeros((1, 128), F32)
    hsend[:, pl.ds(0, 16)] = hid_gain[...]
    hsend[:, pl.ds(16, 16)] = hid_bias[...]

    wait_in(wrecv.at[pl.ds(0, 7), 0, pl.ds(0, 32)], 2)
    send(wrecv.at[:, core, pl.ds(0, 32)], wrecv.at[:, core, pl.ds(0, 32)], 17, sibling)
    wait_in(zrecv, 0)
    zn = norm(zrecv[...].astype(F32).reshape(128, RES), gain_col, bias_col).astype(BF16)
    wait_in(mrecv, 13)
    masking = jnp.concatenate([mrecv[pl.ds(kc, 1), :] for kc in range(4)], axis=1)
    wait_in(wrecv.at[:, 0, pl.ds(0, 32)], 17)

    def operand(side):
        opened = sigmoid(nn(wrecv[:, side, pl.ds(0, 16)].reshape(128, 128), zn))
        value = nn(wrecv[:, side, pl.ds(16, 16)].reshape(128, 128), zn)
        return opened * value * masking

    def swap_f(sent, received, sem):
        def one(k):
            x2, z2 = rem(x + 2 * rem(k + 1, 2), 4), to_z(div(k, 2))
            send(sent.at[f_of(x2, z2)], received.at[f], sem, place(x2, z2))
        each(0, 15, one)
        received[f] = sent[f]

    def swap_y(sent, slot, sem):
        each(0, 7, lambda k: send(sent.at[to_y(k)], slot, sem, dev_y(to_y(k))))

    right = operand(1).reshape(16, 8, RES)
    for kh in range(2):
        at = kh * 256
        rsend[kh] = jnp.concatenate([right[:, :, at:at + 128], right[:, :, at + 128:at + 256]], axis=1).astype(BF16)
        swap_f(rsend.at[kh], rrecv.at[kh], 4 + 15 * kh)
    left = operand(0)
    for lc in range(4):
        work[lc, pl.ds(0, 128), :] = left[:, lc * 128:lc * 128 + 128]
    for lc in range(4):
        for h in range(8):
            lsend[h, :, pl.ds(lc * 128, 128)] = work[lc, pl.ds(h, 16, stride=8), :].astype(BF16)
    swap_y(lsend, lmid.at[y], 14)
    lmid[y] = lsend[y]
    each(0, 4, lambda k: send(hsend, hrecv.at[ch], 16, place(to_x(k), z6)))
    along_x(hsend, hrecv.at[ch], 16)
    hrecv[ch] = hsend[...]

    wait_in(wrecv.at[pl.ds(0, 7), 0, pl.ds(32, 16)], 3)
    send(wrecv.at[:, core, pl.ds(32, 16)], wrecv.at[:, core, pl.ds(32, 16)], 1, sibling)
    wait_in(wrecv.at[:, 0, pl.ds(32, 16)], 1)
    gate = sigmoid(nn(wrecv[:, 0, pl.ds(32, 16)].reshape(128, 128), zn)).T.reshape(8, 4, 2, 8, 128)
    for yy in range(8):
        for cc in range(2):
            gsend[yy * 2 + cc] = gate[yy, :, cc].reshape(32, 128).astype(BF16)

    def gate_b(k):
        y2, core2 = to_y(div(k, 2)), rem(core + 1 + k, 2)
        send(gsend.at[y2 * 2 + core2], g1.at[b], 5, ((y2 * 4 + z_lo) * 2 + core2, ch))

    each(0, 15, gate_b)
    g1[b] = gsend[b]

    def spread_right(kh):
        wait_in(rrecv.at[kh, pl.ds(0, 15)], 4 + 15 * kh)
        work[kh, pl.ds(0, 256), :] = rrecv[kh].astype(F32).reshape(256, 128)
        for h in range(8):
            for lc in range(2):
                rrows[kh, h, :, pl.ds(lc * 128, 128)] = work[kh, pl.ds(lc * 8 + h, 16, stride=16), :].astype(BF16)
        swap_y(rrows.at[kh], rbuf.at[kh, y, u], 11 + 9 * kh)
        rbuf[kh, y, u] = rrows[kh, y]

    spread_right(0)
    wait_in(lmid.at[pl.ds(0, 7)], 14)
    for lc in range(4):
        work[lc, pl.ds(256, 128), :] = lmid[:, :, pl.ds(lc * 128, 128)].astype(F32).reshape(128, 128)
    for g in range(16):
        for lc in range(2):
            lrows[g, :, pl.ds(lc * 128, 128)] = jnp.concatenate(
                [work[kh * 2 + lc, pl.ds(256 + g, 8, stride=16), :] for kh in range(2)], axis=0).astype(BF16)
    swap_f(lrows, lrecv, 6)
    spread_right(1)

    for kh in range(2):
        wait_in(rbuf.at[0, pl.ds(0, 7), 0], 11 + 9 * kh)
        send(rbuf.at[kh, :, u], rbuf.at[kh, :, u], 15 + 6 * kh, place(x + 1 - 2 * u, z))

    wout_t = nt(eye.astype(BF16), wrecv[:, 1, pl.ds(32, 16)].reshape(128, 128)).astype(BF16)
    wait_in(hrecv.at[pl.ds(0, 7)], 16)
    at_gain = iota((8, 16, 128), 1) == iota((8, 16, 128), 2)
    at_bias = iota((8, 16, 128), 1) + 16 == iota((8, 16, 128), 2)

    def column(where):
        col = jnp.sum(jnp.where(where, hrecv[...], 0.0), 2, keepdims=True)
        return jnp.broadcast_to(col, (8, 16, 128)).reshape(128, 128)

    hg, hb = column(at_gain), column(at_bias)
    lane = iota((256, 256), 0)
    natural = (bits(lane, 5, 2) * 64 + bits(lane, 2, 2) * 16 + bits(lane, 4, 1) * 8
               + bits(lane, 1, 1) * 4 + bits(lane, 7, 1) * 2 + bits(lane, 0, 1))
    perm = (natural == iota((256, 256), 1)).astype(BF16)

    wait_in(lrecv.at[pl.ds(0, 15)], 6)
    for lc in range(2):
        work[2 + lc, pl.ds(0, 256), :] = lrecv[:, :, pl.ds(lc * 128, 128)].astype(F32).reshape(256, 128)
    for kh in range(2):
        for yy in range(8):
            for lc in range(2):
                lbuf[kh, yy, core, :, pl.ds(lc * 128, 128)] = work[2 + lc, pl.ds(kh * 8 + yy, 16, stride=16), :].astype(BF16)
    send(lbuf.at[:, :, core], lbuf.at[:, :, core], 12, sibling)
    wait_in(rbuf.at[0, :, 0], 15)
    wait_in(rbuf.at[1, :, 0], 21)
    wait_in(lbuf.at[:, :, 0], 12)
    tri = nt(rbuf[0].reshape(256, 256), lbuf[0].reshape(256, 256)) + nt(rbuf[1].reshape(256, 256), lbuf[1].reshape(256, 256))
    tsend[...] = tri.astype(BF16).reshape(8, 2, 16, 256)

    for v in range(2):
        each(0, 7, lambda k: send(tsend.at[to_y(k), v], t1.at[v, y], 8 + v, dev_y(to_y(k))))
        t1[v, y] = tsend[y, v]

    wait_in(g1.at[pl.ds(0, 15)], 5)
    work[2, :, :] = g1[...].astype(F32).reshape(512, 128)
    for j in range(32):
        lo, high, parity, low = j % 16 // 4, j % 4 // 2, j // 16, j % 2
        g2send[j] = work[2, pl.ds(lo * 8 + high * 4 + parity * 2 + low, 16, stride=32), :].astype(BF16)

    def gate_e(k):
        x2, z2 = to_x(rem(k, 4)), to_z(div(k, 4))
        send(g2send.at[rem(x2, 2) * 16 + f_of(x2, z2)], g2.at[e], 7, place(x2, z2))

    each(0, 31, gate_e)
    g2[e] = g2send[e]

    for v in range(2):
        wait_in(t1.at[v, pl.ds(0, 7)], 8 + v)
        for lc in range(2):
            work[lc, pl.ds(0, 128), :] = t1[v, :, :, pl.ds(lc * 128, 128)].astype(F32).reshape(128, 128)
        for j in range(16):
            t2send[v * 16 + j] = jnp.concatenate(
                [work[lc, pl.ds(j, 8, stride=16), :] for lc in range(2)], axis=0).astype(BF16)
        w = rem(u + v, 2)

        def forward(k):
            x2, z2 = rem(x + 2 - w + rem(k, 2) * (4 * w - 2), 4), to_z(div(k, 2))
            send(t2send.at[v * 16 + f_of(x2, z2)], t2.at[e], 10, place(x2, z2))

        each(0, 15, forward)

        @pl.when(w == 1)
        def _():
            forward(15)

        @pl.when(w == 0)
        def _():
            t2[e] = t2send[v * 16 + f]

    wait_in(g2.at[pl.ds(0, 31)], 7)
    work[2, :, :] = g2[...].astype(F32).reshape(512, 128)
    gate_t = jnp.concatenate(
        [work[2, pl.ds(uu * 256 + bb, 16, stride=16), :] for uu in range(2) for bb in range(16)], axis=0).T

    wait_in(t2.at[pl.ds(0, 31)], 10)
    tiles = t2[...].astype(F32).reshape(2, 16, 2, 8, 128)
    for lt in range(2):
        parts = []
        for uu in range(2):
            tri_ln = norm(tiles[uu, :, lt].reshape(128, 128), hg, hb).astype(BF16)
            at = uu * 256 + lt * 128
            parts.append((nn(wout_t, tri_ln) * gate_t[:, at:at + 128]).astype(BF16))
        update = nn(jnp.concatenate(parts, axis=1), perm)
        usend[lt] = update.astype(BF16).reshape(8, 16, 256)

        def last(k):
            x2, half = to_x(div(k, 2)), rem(z_hi + k, 2)
            send(usend.at[lt, x2 * 2 + half], out.at[e_ch, :, pl.ds(lt * 256, 256)], 18, place(x2, e_lo + 4 * half))

        each(0, 8, last)

    wait_out(zsend, 0)
    wait_out(wrecv.at[:, 0, pl.ds(32, 16)], 1)
    wait_out(wrecv.at[pl.ds(0, 7), 0, pl.ds(0, 32)], 2)
    wait_out(wrecv.at[pl.ds(0, 7), 0, pl.ds(32, 16)], 3)
    wait_out(rsend.at[0, pl.ds(0, 15)], 4)
    wait_out(rsend.at[1, pl.ds(0, 15)], 19)
    wait_out(lsend.at[pl.ds(0, 7)], 14)
    wait_out(gsend.at[pl.ds(0, 15)], 5)
    wait_out(lrows.at[pl.ds(0, 15)], 6)
    wait_out(g2send.at[pl.ds(0, 31)], 7)
    wait_out(t1.at[0, pl.ds(0, 7)], 8)
    wait_out(t1.at[1, pl.ds(0, 7)], 9)
    wait_out(t2send.at[pl.ds(0, 31)], 10)
    wait_out(rrows.at[0, pl.ds(0, 7)], 11)
    wait_out(rrows.at[1, pl.ds(0, 7)], 20)
    wait_out(lbuf.at[:, :, 0], 12)
    wait_out(msend, 13)
    wait_out(rbuf.at[0, :, 0], 15)
    wait_out(rbuf.at[1, :, 0], 21)
    wait_out(hrecv.at[pl.ds(0, 7)], 16)
    wait_out(wrecv.at[:, 0, pl.ds(0, 32)], 17)
    wait_out(usend, 18)
    wait_in(out, 18)


def body(pair, pair_mask, in_gain, in_bias, ab_weight, hid_gain, hid_bias, out_weight, gate_weight):
    rows = pair.shape[1]
    scratch = [
        ((16, rows, RES), BF16), ((rows, RES), jnp.int32), ((2, 48, 128), BF16),
        ((1, CH), F32), ((1, CH), F32), ((1, 16), F32), ((1, 16), F32),
        ((4, 512, 128), F32),
        ((8, 16, RES), BF16), ((8, 16, RES), BF16),
        ((8, 2, 48, 128), BF16),
        ((1, 128), F32), ((8, 1, 128), F32),
        ((8, 128), F32), ((8, 128), F32),
        ((2, 16, 16, 128), BF16), ((2, 16, 16, 128), BF16), ((2, 8, 16, 256), BF16), ((2, 8, 2, 16, 256), BF16),
        ((8, 16, RES), BF16), ((8, 16, RES), BF16), ((16, 16, 256), BF16), ((16, 16, 256), BF16), ((2, 8, 2, 16, 256), BF16),
        ((8, 2, 16, 256), BF16), ((2, 8, 16, 256), BF16),
        ((32, 16, 128), BF16), ((32, 16, 128), BF16),
        ((16, 32, 128), BF16), ((16, 32, 128), BF16),
        ((32, 16, 128), BF16), ((32, 16, 128), BF16),
        ((2, 8, 16, 256), BF16),
    ]
    swapped = pl.pallas_call(
        kernel,
        out_shape=jax.ShapeDtypeStruct((8, 16, RES), BF16),
        in_specs=[pl.BlockSpec(memory_space=pltpu.HBM)] * 9,
        out_specs=pl.BlockSpec(memory_space=pltpu.VMEM),
        scratch_shapes=[pltpu.VMEM(shape, kind) for shape, kind in scratch]
        + [pltpu.SemaphoreType.DMA((9,)), pltpu.SemaphoreType.DMA((22,)), pltpu.SemaphoreType.DMA((22,))],
        compiler_params=pltpu.CompilerParams(
            collective_id=0, has_side_effects=True, vmem_limit_bytes=VMEM_LIMIT),
    )(pair, pair_mask, jnp.swapaxes(ab_weight, 1, 2).reshape(2, 32, CH), in_gain.reshape(1, CH), in_bias.reshape(1, CH),
      gate_weight.T, out_weight, hid_gain.reshape(1, 16), hid_bias.reshape(1, 16))
    return jnp.swapaxes(swapped, 0, 1)


def solution(mesh):
    placed = (
        P("ch", "dap", None),
        P("dap", None),
        P(),
        P(),
        P(None, None, "ch"),
        P("ch"),
        P("ch"),
        P("ch", None),
        P(None, "ch"),
    )
    return jax.shard_map(
        body, mesh=mesh, in_specs=placed, out_specs=P("ch", "dap", None), check_vma=False
    )
```

```python
import jax
import jax.numpy as jnp
from jax import lax
from jax.experimental import pallas as pl
from jax.experimental.pallas import tpu as pltpu
from jax.sharding import PartitionSpec as P

CH = 128
RES = 512
EPS = 1e-05
VMEM_LIMIT = 62 * 1024 * 1024
MESH = pl.DeviceIdType.MESH
F32 = jnp.float32
BF16 = jnp.bfloat16


def nt(a, b):
    return lax.dot_general(a, b, (((1,), (1,)), ((), ())), preferred_element_type=F32)


def nn(a, b):
    return lax.dot_general(a, b, (((1,), (0,)), ((), ())), preferred_element_type=F32)


def iota(shape, dim):
    return lax.broadcasted_iota(jnp.int32, shape, dim)


def bits(value, low, count):
    return lax.shift_right_logical(value, low) & ((1 << count) - 1)


def sigmoid(x):
    return 1.0 / (1.0 + jnp.exp(-x))


def norm(values, gain, bias):
    mean = jnp.sum(values, 0, keepdims=True) * (1.0 / CH)
    square = jnp.sum(values * values, 0, keepdims=True) * (1.0 / CH)
    var = square - mean * mean
    return (values - mean) * lax.rsqrt(var + EPS) * gain + bias


def each(first, last, body):
    def step(k, carry):
        body(k)
        return carry
    lax.fori_loop(first, last, step, 0, unroll=True)


def far(n, top):
    return top + lax.div(n + 1, 2) * (1 - 2 * lax.rem(n, 2))


def kernel(pair_in, mask_in, ab_in, gain_in, bias_in, gate_in, out_in, hid_gain_in, hid_bias_in, out,
           pair, mask, wsend, gain, bias, hid_gain, hid_bias,
           work, zsend, zrecv, wrecv, hsend, hrecv, msend, mrecv,
           rsend, rrecv, rrows, rbuf, lsend, lmid, lrows, lrecv, lbuf, tsend, t1, t2send, t2, gsend, g1, g2send, g2, usend,
           lsem, ssem, rsem):
    div, rem = lax.div, lax.rem
    dap = lax.axis_index("dap")
    ch = lax.axis_index("ch")
    x, z_hi = div(ch, 2), rem(ch, 2)
    y, z_lo, core = div(dap, 8), rem(div(dap, 2), 4), rem(dap, 2)
    z = z_hi * 4 + z_lo
    b = y * 2 + core
    e_lo, s = rem(z + 2, 4), div(rem(z + 6, 8), 4)
    e_ch = 2 * x + s
    u = rem(x, 2)
    f = e_lo * 4 + div(x, 2) * 2 + s
    e = u * 16 + f

    def place(x2, z2):
        return ((y * 4 + rem(z2, 4)) * 2 + core, x2 * 2 + div(z2, 4))

    def f_of(x2, z2):
        return rem(z2 + 2, 4) * 4 + div(x2, 2) * 2 + div(rem(z2 + 6, 8), 4)

    def dev_y(y2):
        return ((y2 * 4 + z_lo) * 2 + core, ch)

    sibling = (dap + 1 - 2 * core, ch)

    def send(src, dst, sem, device):
        pltpu.make_async_remote_copy(
            src_ref=src, dst_ref=dst, send_sem=ssem.at[sem], recv_sem=rsem.at[sem],
            device_id=device, device_id_type=MESH).start()

    def wait_in(ref, sem):
        pltpu.make_async_copy(ref, ref, rsem.at[sem]).wait()

    def wait_out(ref, sem):
        pltpu.make_async_copy(ref, ref, ssem.at[sem]).wait()

    def to_x(k):
        return rem(x + far(k, 2), 4)

    def to_y(k):
        return rem(y + far(k, 4), 8)

    def to_z(k):
        return rem(z + far(k, 4), 8)

    loads = [
        pltpu.make_async_copy(source, target, lsem.at[i]) for i, (source, target) in enumerate((
            (pair_in, pair), (mask_in, mask), (ab_in, wsend.at[:, pl.ds(0, 32)]),
            (gate_in, wsend.at[0, pl.ds(32, 16)]), (out_in, wsend.at[1, pl.ds(32, 16)]),
            (gain_in, gain), (bias_in, bias), (hid_gain_in, hid_gain), (hid_bias_in, hid_bias)))
    ]
    for load in loads:
        load.start()

    barrier = pltpu.get_barrier_semaphore()

    def greet(device):
        pl.semaphore_signal(barrier, inc=1, device_id=device, device_id_type=MESH)

    greet(dev_y(rem(y + 4, 8)))
    each(0, 8, lambda k: greet(place(to_x(div(k, 2)), rem(z + 2 + 4 * rem(k, 2), 8))))
    each(1, 7, lambda k: greet(dev_y(to_y(k))))
    each(0, 3, lambda k: greet(place(to_x(k), z)))
    each(0, 2, lambda k: greet(place(x, rem(z + 1 + 6 * k, 8))))
    greet(sibling)

    for load in loads:
        load.wait()
    for kc in range(4):
        work[kc, pl.ds(0, 128), :] = pair[:, :, pl.ds(kc * 128, 128)].astype(F32).reshape(128, 128)
    for kc in range(4):
        for r in range(8):
            zsend[r, :, pl.ds(kc * 128, 128)] = work[kc, pl.ds(r, 16, stride=8), :].astype(BF16)
    own_mask = mask[pl.ds(ch, 1), :].astype(F32)
    for kc in range(4):
        msend[pl.ds(kc, 1), :] = own_mask[:, kc * 128:kc * 128 + 128]

    pl.semaphore_wait(barrier, 21)

    def first(k):
        x2, s2 = to_x(div(k, 2)), rem(s + k, 2)
        send(zsend.at[x2 * 2 + s2], zrecv.at[ch], 0, place(x2, rem(z_lo + 2 + 4 * s2, 8)))

    z6 = 4 * (1 - z_hi) + 2 * (1 - div(z_lo, 2)) + rem(z_lo, 2)
    crossed = x * 2 + 1 - z_hi

    def along_x(src, dst, sem):
        each(0, 3, lambda k: send(src, dst, sem, place(to_x(k), z)))

    each(0, 4, lambda k: send(wsend.at[core, pl.ds(0, 32)], wrecv.at[ch, core, pl.ds(0, 32)], 2, place(to_x(k), z6)))
    along_x(wsend.at[core, pl.ds(0, 32)], wrecv.at[ch, core, pl.ds(0, 32)], 2)
    each(0, 8, first)
    each(0, 4, lambda k: send(wsend.at[core, pl.ds(32, 16)], wrecv.at[ch, core, pl.ds(32, 16)], 3, place(to_x(k), z6)))
    along_x(wsend.at[core, pl.ds(32, 16)], wrecv.at[ch, core, pl.ds(32, 16)], 3)
    send(msend, mrecv, 13, place(x, rem(z_lo + 2 + 4 * z_hi, 8)))
    wrecv[ch, core] = wsend[core]

    eye = iota((128, 128), 0) == iota((128, 128), 1)
    gain_col = jnp.sum(jnp.where(eye, gain[...], 0.0), 1, keepdims=True)
    bias_col = jnp.sum(jnp.where(eye, bias[...], 0.0), 1, keepdims=True)
    hsend[...] = jnp.zeros((1, 128), F32)
    hsend[:, pl.ds(0, 16)] = hid_gain[...]
    hsend[:, pl.ds(16, 16)] = hid_bias[...]

    wait_in(wrecv.at[pl.ds(0, 7), 0, pl.ds(0, 32)], 2)
    send(wrecv.at[:, core, pl.ds(0, 32)], wrecv.at[:, core, pl.ds(0, 32)], 17, sibling)
    wait_in(zrecv, 0)
    zn = norm(zrecv[...].astype(F32).reshape(128, RES), gain_col, bias_col).astype(BF16)
    wait_in(mrecv, 13)
    masking = jnp.concatenate([mrecv[pl.ds(kc, 1), :] for kc in range(4)], axis=1)
    wait_in(wrecv.at[:, 0, pl.ds(0, 32)], 17)

    def operand(side):
        opened = sigmoid(nn(wrecv[:, side, pl.ds(0, 16)].reshape(128, 128), zn))
        value = nn(wrecv[:, side, pl.ds(16, 16)].reshape(128, 128), zn)
        return opened * value * masking

    def swap_f(sent, received, sem):
        def one(k):
            x2, z2 = rem(x + 2 * rem(k + 1, 2), 4), to_z(div(k, 2))
            send(sent.at[f_of(x2, z2)], received.at[f], sem, place(x2, z2))
        each(0, 15, one)
        received[f] = sent[f]

    def swap_y(sent, slot, sem):
        each(0, 7, lambda k: send(sent.at[to_y(k)], slot, sem, dev_y(to_y(k))))

    right = operand(1).reshape(16, 8, RES)

    def swap_right(kh):
        at = kh * 256
        rsend[kh] = jnp.concatenate([right[:, :, at:at + 128], right[:, :, at + 128:at + 256]], axis=1).astype(BF16)
        swap_f(rsend.at[kh], rrecv.at[kh], 4 + 15 * kh)

    swap_right(0)
    left = operand(0)
    for lc in range(4):
        work[lc, pl.ds(0, 128), :] = left[:, lc * 128:lc * 128 + 128]
    for lc in range(4):
        for h in range(8):
            lsend[h, :, pl.ds(lc * 128, 128)] = work[lc, pl.ds(h, 16, stride=8), :].astype(BF16)
    swap_y(lsend, lmid.at[y], 14)
    lmid[y] = lsend[y]
    swap_right(1)
    hrecv[ch] = hsend[...]

    wait_in(wrecv.at[pl.ds(0, 7), 0, pl.ds(32, 16)], 3)
    send(wrecv.at[:, core, pl.ds(32, 16)], wrecv.at[:, core, pl.ds(32, 16)], 1, sibling)
    wait_in(wrecv.at[:, 0, pl.ds(32, 16)], 1)
    gate = sigmoid(nn(wrecv[:, 0, pl.ds(32, 16)].reshape(128, 128), zn)).T.reshape(8, 4, 2, 8, 128)
    for yy in range(8):
        for cc in range(2):
            gsend[yy * 2 + cc] = gate[yy, :, cc].reshape(32, 128).astype(BF16)

    def gate_b(k):
        y2, core2 = to_y(div(k, 2)), rem(core + 1 + k, 2)
        send(gsend.at[y2 * 2 + core2], g1.at[b], 5, ((y2 * 4 + z_lo) * 2 + core2, ch))

    each(0, 15, gate_b)
    g1[b] = gsend[b]

    each(0, 4, lambda k: send(hsend, hrecv.at[ch], 16, place(to_x(k), z6)))
    along_x(hsend, hrecv.at[ch], 16)

    def spread_right(kh):
        wait_in(rrecv.at[kh, pl.ds(0, 15)], 4 + 15 * kh)
        work[kh, pl.ds(0, 256), :] = rrecv[kh].astype(F32).reshape(256, 128)
        for h in range(8):
            for lc in range(2):
                rrows[kh, h, :, pl.ds(lc * 128, 128)] = work[kh, pl.ds(lc * 8 + h, 16, stride=16), :].astype(BF16)
        if kh == 1:
            each(0, 8, lambda k: send(rrows.at[1, to_y(k)], rbuf.at[1, y, u], 20, (dev_y(to_y(k))[0], ch + 2 - 4 * u)))
        swap_y(rrows.at[kh], rbuf.at[kh, y, u], 11 + 9 * kh)
        rbuf[kh, y, u] = rrows[kh, y]

    spread_right(0)
    wait_in(lmid.at[pl.ds(0, 7)], 14)
    for lc in range(4):
        work[lc, pl.ds(256, 128), :] = lmid[:, :, pl.ds(lc * 128, 128)].astype(F32).reshape(128, 128)
    for g in range(16):
        for lc in range(2):
            lrows[g, :, pl.ds(lc * 128, 128)] = jnp.concatenate(
                [work[kh * 2 + lc, pl.ds(256 + g, 8, stride=16), :] for kh in range(2)], axis=0).astype(BF16)
    swap_f(lrows, lrecv, 6)
    spread_right(1)

    wait_in(rbuf.at[0, pl.ds(0, 7), 0], 11)
    send(rbuf.at[0, :, u], rbuf.at[0, :, u], 15, place(x + 1 - 2 * u, z))

    wout_t = nt(eye.astype(BF16), wrecv[:, 1, pl.ds(32, 16)].reshape(128, 128)).astype(BF16)
    wait_in(hrecv.at[pl.ds(0, 7)], 16)
    at_gain = iota((8, 16, 128), 1) == iota((8, 16, 128), 2)
    at_bias = iota((8, 16, 128), 1) + 16 == iota((8, 16, 128), 2)

    def column(where):
        col = jnp.sum(jnp.where(where, hrecv[...], 0.0), 2, keepdims=True)
        return jnp.broadcast_to(col, (8, 16, 128)).reshape(128, 128)

    hg, hb = column(at_gain), column(at_bias)
    lane = iota((256, 256), 0)
    natural = (bits(lane, 5, 2) * 64 + bits(lane, 2, 2) * 16 + bits(lane, 4, 1) * 8
               + bits(lane, 1, 1) * 4 + bits(lane, 7, 1) * 2 + bits(lane, 0, 1))
    perm = (natural == iota((256, 256), 1)).astype(BF16)

    wait_in(lrecv.at[pl.ds(0, 15)], 6)
    for lc in range(2):
        work[2 + lc, pl.ds(0, 256), :] = lrecv[:, :, pl.ds(lc * 128, 128)].astype(F32).reshape(256, 128)
    for kh in range(2):
        for yy in range(8):
            for lc in range(2):
                lbuf[kh, yy, core, :, pl.ds(lc * 128, 128)] = work[2 + lc, pl.ds(kh * 8 + yy, 16, stride=16), :].astype(BF16)
    send(lbuf.at[:, :, core], lbuf.at[:, :, core], 12, sibling)
    wait_in(rbuf.at[0, :, 0], 15)
    wait_in(rrecv.at[:, pl.ds(0, 15)], 20)
    wait_in(lbuf.at[:, :, 0], 12)
    tri = nt(rbuf[0].reshape(256, 256), lbuf[0].reshape(256, 256)) + nt(rbuf[1].reshape(256, 256), lbuf[1].reshape(256, 256))
    tsend[...] = tri.astype(BF16).reshape(8, 2, 16, 256)

    for v in range(2):
        each(0, 7, lambda k: send(tsend.at[to_y(k), v], t1.at[v, y], 8 + v, dev_y(to_y(k))))
        t1[v, y] = tsend[y, v]

    wait_in(g1.at[pl.ds(0, 15)], 5)
    work[2, :, :] = g1[...].astype(F32).reshape(512, 128)
    for j in range(32):
        lo, high, parity, low = j % 16 // 4, j % 4 // 2, j // 16, j % 2
        g2send[j] = work[2, pl.ds(lo * 8 + high * 4 + parity * 2 + low, 16, stride=32), :].astype(BF16)

    def gate_e(k):
        x2, z2 = to_x(rem(k, 4)), to_z(div(k, 4))
        send(g2send.at[rem(x2, 2) * 16 + f_of(x2, z2)], g2.at[e], 7, place(x2, z2))

    each(0, 31, gate_e)
    g2[e] = g2send[e]

    for v in range(2):
        wait_in(t1.at[v, pl.ds(0, 7)], 8 + v)
        for lc in range(2):
            work[lc, pl.ds(0, 128), :] = t1[v, :, :, pl.ds(lc * 128, 128)].astype(F32).reshape(128, 128)
        for j in range(16):
            t2send[v * 16 + j] = jnp.concatenate(
                [work[lc, pl.ds(j, 8, stride=16), :] for lc in range(2)], axis=0).astype(BF16)
        w = rem(u + v, 2)

        def forward(k):
            x2, z2 = rem(x + 2 - w + rem(k, 2) * (4 * w - 2), 4), to_z(div(k, 2))
            send(t2send.at[v * 16 + f_of(x2, z2)], t2.at[e], 10, place(x2, z2))

        each(0, 15, forward)

        @pl.when(w == 1)
        def _():
            forward(15)

        @pl.when(w == 0)
        def _():
            t2[e] = t2send[v * 16 + f]

    wait_in(g2.at[pl.ds(0, 31)], 7)
    work[2, :, :] = g2[...].astype(F32).reshape(512, 128)
    gate_t = jnp.concatenate(
        [work[2, pl.ds(uu * 256 + bb, 16, stride=16), :] for uu in range(2) for bb in range(16)], axis=0).T

    wait_in(t2.at[pl.ds(0, 31)], 10)
    tiles = t2[...].astype(F32).reshape(2, 16, 2, 8, 128)
    for lt in range(2):
        parts = []
        for uu in range(2):
            tri_ln = norm(tiles[uu, :, lt].reshape(128, 128), hg, hb).astype(BF16)
            at = uu * 256 + lt * 128
            parts.append((nn(wout_t, tri_ln) * gate_t[:, at:at + 128]).astype(BF16))
        update = nn(jnp.concatenate(parts, axis=1), perm)
        usend[lt] = update.astype(BF16).reshape(8, 16, 256)

        def last(k):
            x2, half = to_x(div(k, 2)), rem(z_hi + k, 2)
            send(usend.at[lt, x2 * 2 + half], out.at[e_ch, :, pl.ds(lt * 256, 256)], 18, place(x2, e_lo + 4 * half))

        each(0, 8, last)

    wait_out(zsend, 0)
    wait_out(wrecv.at[:, 0, pl.ds(32, 16)], 1)
    wait_out(wrecv.at[pl.ds(0, 7), 0, pl.ds(0, 32)], 2)
    wait_out(wrecv.at[pl.ds(0, 7), 0, pl.ds(32, 16)], 3)
    wait_out(rsend.at[0, pl.ds(0, 15)], 4)
    wait_out(rsend.at[1, pl.ds(0, 15)], 19)
    wait_out(lsend.at[pl.ds(0, 7)], 14)
    wait_out(gsend.at[pl.ds(0, 15)], 5)
    wait_out(lrows.at[pl.ds(0, 15)], 6)
    wait_out(g2send.at[pl.ds(0, 31)], 7)
    wait_out(t1.at[0, pl.ds(0, 7)], 8)
    wait_out(t1.at[1, pl.ds(0, 7)], 9)
    wait_out(t2send.at[pl.ds(0, 31)], 10)
    wait_out(rrows.at[0, pl.ds(0, 7)], 11)
    wait_out(rrecv.at[:, pl.ds(0, 15)], 20)
    wait_out(lbuf.at[:, :, 0], 12)
    wait_out(msend, 13)
    wait_out(rbuf.at[0, :, 0], 15)
    wait_out(hrecv.at[pl.ds(0, 7)], 16)
    wait_out(wrecv.at[:, 0, pl.ds(0, 32)], 17)
    wait_out(usend, 18)
    wait_in(out, 18)


def body(pair, pair_mask, in_gain, in_bias, ab_weight, hid_gain, hid_bias, out_weight, gate_weight):
    rows = pair.shape[1]
    scratch = [
        ((16, rows, RES), BF16), ((rows, RES), jnp.int32), ((2, 48, 128), BF16),
        ((1, CH), F32), ((1, CH), F32), ((1, 16), F32), ((1, 16), F32),
        ((4, 512, 128), F32),
        ((8, 16, RES), BF16), ((8, 16, RES), BF16),
        ((8, 2, 48, 128), BF16),
        ((1, 128), F32), ((8, 1, 128), F32),
        ((8, 128), F32), ((8, 128), F32),
        ((2, 16, 16, 128), BF16), ((2, 16, 16, 128), BF16), ((2, 8, 16, 256), BF16), ((2, 8, 2, 16, 256), BF16),
        ((8, 16, RES), BF16), ((8, 16, RES), BF16), ((16, 16, 256), BF16), ((16, 16, 256), BF16), ((2, 8, 2, 16, 256), BF16),
        ((8, 2, 16, 256), BF16), ((2, 8, 16, 256), BF16),
        ((32, 16, 128), BF16), ((32, 16, 128), BF16),
        ((16, 32, 128), BF16), ((16, 32, 128), BF16),
        ((32, 16, 128), BF16), ((32, 16, 128), BF16),
        ((2, 8, 16, 256), BF16),
    ]
    swapped = pl.pallas_call(
        kernel,
        out_shape=pltpu.VMEM((8, 16, RES), BF16),
        in_specs=[pl.BlockSpec(memory_space=pltpu.HBM)] * 9,
        out_specs=pl.BlockSpec(memory_space=pltpu.VMEM),
        scratch_shapes=[pltpu.VMEM(shape, kind) for shape, kind in scratch]
        + [pltpu.SemaphoreType.DMA((9,)), pltpu.SemaphoreType.DMA((22,)), pltpu.SemaphoreType.DMA((22,))],
        compiler_params=pltpu.CompilerParams(
            collective_id=0, has_side_effects=True, vmem_limit_bytes=VMEM_LIMIT),
    )(pair, pair_mask, jnp.swapaxes(ab_weight, 1, 2).reshape(2, 32, CH), in_gain.reshape(1, CH), in_bias.reshape(1, CH),
      gate_weight.T, out_weight, hid_gain.reshape(1, 16), hid_bias.reshape(1, 16))
    return jnp.swapaxes(swapped, 0, 1)


def solution(mesh):
    placed = (
        P("ch", "dap", None),
        P("dap", None),
        P(),
        P(),
        P(None, None, "ch"),
        P("ch"),
        P("ch"),
        P("ch", None),
        P(None, "ch"),
    )
    return jax.shard_map(
        body, mesh=mesh, in_specs=placed, out_specs=P("ch", "dap", None), check_vma=False
    )
```

```python
import jax
import jax.numpy as jnp
from jax import lax
from jax.experimental import pallas as pl
from jax.experimental.pallas import tpu as pltpu
from jax.sharding import PartitionSpec as P

CH = 128
RES = 512
EPS = 1e-05
VMEM_LIMIT = 62 * 1024 * 1024
MESH = pl.DeviceIdType.MESH
F32 = jnp.float32
BF16 = jnp.bfloat16


def nt(a, b):
    return lax.dot_general(a, b, (((1,), (1,)), ((), ())), preferred_element_type=F32)


def nn(a, b):
    return lax.dot_general(a, b, (((1,), (0,)), ((), ())), preferred_element_type=F32)


def iota(shape, dim):
    return lax.broadcasted_iota(jnp.int32, shape, dim)


def bits(value, low, count):
    return lax.shift_right_logical(value, low) & ((1 << count) - 1)


def sigmoid(x):
    return 1.0 / (1.0 + jnp.exp(-x))


def norm(values, gain, bias):
    mean = jnp.sum(values, 0, keepdims=True) * (1.0 / CH)
    square = jnp.sum(values * values, 0, keepdims=True) * (1.0 / CH)
    var = square - mean * mean
    return (values - mean) * lax.rsqrt(var + EPS) * gain + bias


def each(first, last, body):
    def step(k, carry):
        body(k)
        return carry
    lax.fori_loop(first, last, step, 0, unroll=True)


def far(n, top):
    return top + lax.div(n + 1, 2) * (1 - 2 * lax.rem(n, 2))


def kernel(pair_in, mask_in, ab_in, gain_in, bias_in, gate_in, out_in, hid_gain_in, hid_bias_in, out,
           pair, mask, wsend, gain, bias, hid_gain, hid_bias,
           work, zsend, zrecv, wrecv, hsend, hrecv, msend, mrecv,
           rsend, rrecv, rrows, rbuf, lsend, lmid, lrows, lrecv, lbuf, tsend, t1, t2send, t2, gsend, g1, g2send, g2, usend,
           lsem, ssem, rsem):
    div, rem = lax.div, lax.rem
    dap = lax.axis_index("dap")
    ch = lax.axis_index("ch")
    x, z_hi = div(ch, 2), rem(ch, 2)
    y, z_lo, core = div(dap, 8), rem(div(dap, 2), 4), rem(dap, 2)
    z = z_hi * 4 + z_lo
    b = y * 2 + core
    e_lo, s = rem(z + 2, 4), div(rem(z + 6, 8), 4)
    e_ch = 2 * x + s
    u = rem(x, 2)
    f = e_lo * 4 + div(x, 2) * 2 + s
    e = u * 16 + f

    def place(x2, z2):
        return ((y * 4 + rem(z2, 4)) * 2 + core, x2 * 2 + div(z2, 4))

    def f_of(x2, z2):
        return rem(z2 + 2, 4) * 4 + div(x2, 2) * 2 + div(rem(z2 + 6, 8), 4)

    def dev_y(y2):
        return ((y2 * 4 + z_lo) * 2 + core, ch)

    sibling = (dap + 1 - 2 * core, ch)

    def send(src, dst, sem, device):
        pltpu.make_async_remote_copy(
            src_ref=src, dst_ref=dst, send_sem=ssem.at[sem], recv_sem=rsem.at[sem],
            device_id=device, device_id_type=MESH).start()

    def wait_in(ref, sem):
        pltpu.make_async_copy(ref, ref, rsem.at[sem]).wait()

    def wait_out(ref, sem):
        pltpu.make_async_copy(ref, ref, ssem.at[sem]).wait()

    def to_x(k):
        return rem(x + far(k, 2), 4)

    def to_y(k):
        return rem(y + far(k, 4), 8)

    def to_z(k):
        return rem(z + far(k, 4), 8)

    loads = [
        pltpu.make_async_copy(source, target, lsem.at[i]) for i, (source, target) in enumerate((
            (pair_in, pair), (mask_in, mask), (ab_in, wsend.at[:, pl.ds(0, 32)]),
            (gate_in, wsend.at[0, pl.ds(32, 16)]), (out_in, wsend.at[1, pl.ds(32, 16)]),
            (gain_in, gain), (bias_in, bias), (hid_gain_in, hid_gain), (hid_bias_in, hid_bias)))
    ]
    for load in loads:
        load.start()

    barrier = pltpu.get_barrier_semaphore()

    def greet(device):
        pl.semaphore_signal(barrier, inc=1, device_id=device, device_id_type=MESH)

    greet(dev_y(rem(y + 4, 8)))
    each(0, 8, lambda k: greet(place(to_x(div(k, 2)), rem(z + 2 + 4 * rem(k, 2), 8))))
    each(1, 7, lambda k: greet(dev_y(to_y(k))))
    each(0, 3, lambda k: greet(place(to_x(k), z)))
    each(0, 2, lambda k: greet(place(x, rem(z + 1 + 6 * k, 8))))
    greet(sibling)

    for load in loads:
        load.wait()
    for kc in range(4):
        work[kc, pl.ds(0, 128), :] = pair[:, :, pl.ds(kc * 128, 128)].astype(F32).reshape(128, 128)
    for kc in range(4):
        for r in range(8):
            zsend[r, :, pl.ds(kc * 128, 128)] = work[kc, pl.ds(r, 16, stride=8), :].astype(BF16)
    own_mask = mask[pl.ds(ch, 1), :].astype(F32)
    for kc in range(4):
        msend[pl.ds(kc, 1), :] = own_mask[:, kc * 128:kc * 128 + 128]

    pl.semaphore_wait(barrier, 21)

    def first(k):
        x2, s2 = to_x(div(k, 2)), rem(s + k, 2)
        send(zsend.at[x2 * 2 + s2], zrecv.at[ch], 0, place(x2, rem(z_lo + 2 + 4 * s2, 8)))

    z6 = 4 * (1 - z_hi) + 2 * (1 - div(z_lo, 2)) + rem(z_lo, 2)
    crossed = x * 2 + 1 - z_hi

    def along_x(src, dst, sem):
        each(0, 3, lambda k: send(src, dst, sem, place(to_x(k), z)))

    each(0, 4, lambda k: send(wsend.at[core, pl.ds(0, 32)], wrecv.at[ch, core, pl.ds(0, 32)], 2, place(to_x(k), z6)))
    along_x(wsend.at[core, pl.ds(0, 32)], wrecv.at[ch, core, pl.ds(0, 32)], 2)
    each(0, 8, first)
    each(0, 4, lambda k: send(wsend.at[core, pl.ds(32, 16)], wrecv.at[ch, core, pl.ds(32, 16)], 3, place(to_x(k), z6)))
    along_x(wsend.at[core, pl.ds(32, 16)], wrecv.at[ch, core, pl.ds(32, 16)], 3)
    send(msend, mrecv, 13, place(x, rem(z_lo + 2 + 4 * z_hi, 8)))
    wrecv[ch, core] = wsend[core]

    eye = iota((128, 128), 0) == iota((128, 128), 1)
    gain_col = jnp.sum(jnp.where(eye, gain[...], 0.0), 1, keepdims=True)
    bias_col = jnp.sum(jnp.where(eye, bias[...], 0.0), 1, keepdims=True)
    hsend[...] = jnp.zeros((1, 128), F32)
    hsend[:, pl.ds(0, 16)] = hid_gain[...]
    hsend[:, pl.ds(16, 16)] = hid_bias[...]

    wait_in(wrecv.at[pl.ds(0, 7), 0, pl.ds(0, 32)], 2)
    send(wrecv.at[:, core, pl.ds(0, 32)], wrecv.at[:, core, pl.ds(0, 32)], 17, sibling)
    wait_in(zrecv, 0)
    zn = norm(zrecv[...].astype(F32).reshape(128, RES), gain_col, bias_col).astype(BF16)
    wait_in(mrecv, 13)
    masking = jnp.concatenate([mrecv[pl.ds(kc, 1), :] for kc in range(4)], axis=1)
    wait_in(wrecv.at[:, 0, pl.ds(0, 32)], 17)

    def operand(side):
        opened = sigmoid(nn(wrecv[:, side, pl.ds(0, 16)].reshape(128, 128), zn))
        value = nn(wrecv[:, side, pl.ds(16, 16)].reshape(128, 128), zn)
        return opened * value * masking

    def swap_f(sent, received, sem):
        def one(k):
            x2, z2 = rem(x + 2 * rem(k + 1, 2), 4), to_z(div(k, 2))
            send(sent.at[f_of(x2, z2)], received.at[f], sem, place(x2, z2))
        each(0, 15, one)
        received[f] = sent[f]

    def swap_y(sent, slot, sem):
        each(0, 7, lambda k: send(sent.at[to_y(k)], slot, sem, dev_y(to_y(k))))

    left = operand(0)
    for lc in range(4):
        work[lc, pl.ds(0, 128), :] = left[:, lc * 128:lc * 128 + 128]
    for lc in range(4):
        for h in range(8):
            lsend[h, :, pl.ds(lc * 128, 128)] = work[lc, pl.ds(h, 16, stride=8), :].astype(BF16)
    swap_y(lsend, lmid.at[y], 14)
    lmid[y] = lsend[y]
    right = operand(1).reshape(16, 8, RES)

    def swap_right(kh):
        at = kh * 256
        rsend[kh] = jnp.concatenate([right[:, :, at:at + 128], right[:, :, at + 128:at + 256]], axis=1).astype(BF16)
        swap_f(rsend.at[kh], rrecv.at[kh], 4 + 15 * kh)

    swap_right(0)
    swap_right(1)
    hrecv[ch] = hsend[...]

    wait_in(wrecv.at[pl.ds(0, 7), 0, pl.ds(32, 16)], 3)
    send(wrecv.at[:, core, pl.ds(32, 16)], wrecv.at[:, core, pl.ds(32, 16)], 1, sibling)
    wait_in(wrecv.at[:, 0, pl.ds(32, 16)], 1)
    gate = sigmoid(nn(wrecv[:, 0, pl.ds(32, 16)].reshape(128, 128), zn)).T.reshape(8, 4, 2, 8, 128)
    for yy in range(8):
        for cc in range(2):
            gsend[yy * 2 + cc] = gate[yy, :, cc].reshape(32, 128).astype(BF16)

    def gate_b(k):
        y2, core2 = to_y(div(k, 2)), rem(core + 1 + k, 2)
        send(gsend.at[y2 * 2 + core2], g1.at[b], 5, ((y2 * 4 + z_lo) * 2 + core2, ch))

    each(0, 15, gate_b)
    g1[b] = gsend[b]

    each(0, 4, lambda k: send(hsend, hrecv.at[ch], 16, place(to_x(k), z6)))
    along_x(hsend, hrecv.at[ch], 16)

    def spread_right(kh):
        wait_in(rrecv.at[kh, pl.ds(0, 15)], 4 + 15 * kh)
        work[kh, pl.ds(0, 256), :] = rrecv[kh].astype(F32).reshape(256, 128)
        for h in range(8):
            for lc in range(2):
                rrows[kh, h, :, pl.ds(lc * 128, 128)] = work[kh, pl.ds(lc * 8 + h, 16, stride=16), :].astype(BF16)
        if kh == 1:
            each(0, 8, lambda k: send(rrows.at[1, to_y(k)], rbuf.at[1, y, u], 20, (dev_y(to_y(k))[0], ch + 2 - 4 * u)))
        swap_y(rrows.at[kh], rbuf.at[kh, y, u], 11 + 9 * kh)
        rbuf[kh, y, u] = rrows[kh, y]

    spread_right(0)
    wait_in(lmid.at[pl.ds(0, 7)], 14)
    for lc in range(4):
        work[lc, pl.ds(256, 128), :] = lmid[:, :, pl.ds(lc * 128, 128)].astype(F32).reshape(128, 128)
    for g in range(16):
        for lc in range(2):
            lrows[g, :, pl.ds(lc * 128, 128)] = jnp.concatenate(
                [work[kh * 2 + lc, pl.ds(256 + g, 8, stride=16), :] for kh in range(2)], axis=0).astype(BF16)
    swap_f(lrows, lrecv, 6)
    spread_right(1)

    wait_in(rbuf.at[0, pl.ds(0, 7), 0], 11)
    send(rbuf.at[0, :, u], rbuf.at[0, :, u], 15, place(x + 1 - 2 * u, z))

    wout_t = nt(eye.astype(BF16), wrecv[:, 1, pl.ds(32, 16)].reshape(128, 128)).astype(BF16)
    wait_in(hrecv.at[pl.ds(0, 7)], 16)
    at_gain = iota((8, 16, 128), 1) == iota((8, 16, 128), 2)
    at_bias = iota((8, 16, 128), 1) + 16 == iota((8, 16, 128), 2)

    def column(where):
        col = jnp.sum(jnp.where(where, hrecv[...], 0.0), 2, keepdims=True)
        return jnp.broadcast_to(col, (8, 16, 128)).reshape(128, 128)

    hg, hb = column(at_gain), column(at_bias)
    lane = iota((256, 256), 0)
    natural = (bits(lane, 5, 2) * 64 + bits(lane, 2, 2) * 16 + bits(lane, 4, 1) * 8
               + bits(lane, 1, 1) * 4 + bits(lane, 7, 1) * 2 + bits(lane, 0, 1))
    perm = (natural == iota((256, 256), 1)).astype(BF16)

    wait_in(lrecv.at[pl.ds(0, 15)], 6)
    for lc in range(2):
        work[2 + lc, pl.ds(0, 256), :] = lrecv[:, :, pl.ds(lc * 128, 128)].astype(F32).reshape(256, 128)
    for kh in range(2):
        for yy in range(8):
            for lc in range(2):
                lbuf[kh, yy, core, :, pl.ds(lc * 128, 128)] = work[2 + lc, pl.ds(kh * 8 + yy, 16, stride=16), :].astype(BF16)
    send(lbuf.at[:, :, core], lbuf.at[:, :, core], 12, sibling)
    wait_in(rbuf.at[0, :, 0], 15)
    wait_in(rrecv.at[:, pl.ds(0, 15)], 20)
    wait_in(lbuf.at[:, :, 0], 12)
    tri = nt(rbuf[0].reshape(256, 256), lbuf[0].reshape(256, 256)) + nt(rbuf[1].reshape(256, 256), lbuf[1].reshape(256, 256))
    tsend[...] = tri.astype(BF16).reshape(8, 2, 16, 256)

    for v in range(2):
        each(0, 7, lambda k: send(tsend.at[to_y(k), v], t1.at[v, y], 8 + v, dev_y(to_y(k))))
        t1[v, y] = tsend[y, v]

    wait_in(g1.at[pl.ds(0, 15)], 5)
    work[2, :, :] = g1[...].astype(F32).reshape(512, 128)
    for j in range(32):
        lo, high, parity, low = j % 16 // 4, j % 4 // 2, j // 16, j % 2
        g2send[j] = work[2, pl.ds(lo * 8 + high * 4 + parity * 2 + low, 16, stride=32), :].astype(BF16)

    def gate_e(k):
        x2, z2 = to_x(rem(k, 4)), to_z(div(k, 4))
        send(g2send.at[rem(x2, 2) * 16 + f_of(x2, z2)], g2.at[e], 7, place(x2, z2))

    each(0, 31, gate_e)
    g2[e] = g2send[e]

    for v in range(2):
        wait_in(t1.at[v, pl.ds(0, 7)], 8 + v)
        for lc in range(2):
            work[lc, pl.ds(0, 128), :] = t1[v, :, :, pl.ds(lc * 128, 128)].astype(F32).reshape(128, 128)
        for j in range(16):
            t2send[v * 16 + j] = jnp.concatenate(
                [work[lc, pl.ds(j, 8, stride=16), :] for lc in range(2)], axis=0).astype(BF16)
        w = rem(u + v, 2)

        def forward(k):
            x2, z2 = rem(x + 2 - w + rem(k, 2) * (4 * w - 2), 4), to_z(div(k, 2))
            send(t2send.at[v * 16 + f_of(x2, z2)], t2.at[e], 10, place(x2, z2))

        each(0, 15, forward)

        @pl.when(w == 1)
        def _():
            forward(15)

        @pl.when(w == 0)
        def _():
            t2[e] = t2send[v * 16 + f]

    wait_in(g2.at[pl.ds(0, 31)], 7)
    work[2, :, :] = g2[...].astype(F32).reshape(512, 128)
    gate_t = jnp.concatenate(
        [work[2, pl.ds(uu * 256 + bb, 16, stride=16), :] for uu in range(2) for bb in range(16)], axis=0).T

    wait_in(t2.at[pl.ds(0, 31)], 10)
    tiles = t2[...].astype(F32).reshape(2, 16, 2, 8, 128)
    for lt in range(2):
        parts = []
        for uu in range(2):
            tri_ln = norm(tiles[uu, :, lt].reshape(128, 128), hg, hb).astype(BF16)
            at = uu * 256 + lt * 128
            parts.append((nn(wout_t, tri_ln) * gate_t[:, at:at + 128]).astype(BF16))
        update = nn(jnp.concatenate(parts, axis=1), perm)
        usend[lt] = update.astype(BF16).reshape(8, 16, 256)

        def last(k):
            x2, half = to_x(div(k, 2)), rem(z_hi + k, 2)
            send(usend.at[lt, x2 * 2 + half], out.at[e_ch, :, pl.ds(lt * 256, 256)], 18, place(x2, e_lo + 4 * half))

        each(0, 8, last)

    wait_out(zsend, 0)
    wait_out(wrecv.at[:, 0, pl.ds(32, 16)], 1)
    wait_out(wrecv.at[pl.ds(0, 7), 0, pl.ds(0, 32)], 2)
    wait_out(wrecv.at[pl.ds(0, 7), 0, pl.ds(32, 16)], 3)
    wait_out(rsend.at[0, pl.ds(0, 15)], 4)
    wait_out(rsend.at[1, pl.ds(0, 15)], 19)
    wait_out(lsend.at[pl.ds(0, 7)], 14)
    wait_out(gsend.at[pl.ds(0, 15)], 5)
    wait_out(lrows.at[pl.ds(0, 15)], 6)
    wait_out(g2send.at[pl.ds(0, 31)], 7)
    wait_out(t1.at[0, pl.ds(0, 7)], 8)
    wait_out(t1.at[1, pl.ds(0, 7)], 9)
    wait_out(t2send.at[pl.ds(0, 31)], 10)
    wait_out(rrows.at[0, pl.ds(0, 7)], 11)
    wait_out(rrecv.at[:, pl.ds(0, 15)], 20)
    wait_out(lbuf.at[:, :, 0], 12)
    wait_out(msend, 13)
    wait_out(rbuf.at[0, :, 0], 15)
    wait_out(hrecv.at[pl.ds(0, 7)], 16)
    wait_out(wrecv.at[:, 0, pl.ds(0, 32)], 17)
    wait_out(usend, 18)
    wait_in(out, 18)


def body(pair, pair_mask, in_gain, in_bias, ab_weight, hid_gain, hid_bias, out_weight, gate_weight):
    rows = pair.shape[1]
    scratch = [
        ((16, rows, RES), BF16), ((rows, RES), jnp.int32), ((2, 48, 128), BF16),
        ((1, CH), F32), ((1, CH), F32), ((1, 16), F32), ((1, 16), F32),
        ((4, 512, 128), F32),
        ((8, 16, RES), BF16), ((8, 16, RES), BF16),
        ((8, 2, 48, 128), BF16),
        ((1, 128), F32), ((8, 1, 128), F32),
        ((8, 128), F32), ((8, 128), F32),
        ((2, 16, 16, 128), BF16), ((2, 16, 16, 128), BF16), ((2, 8, 16, 256), BF16), ((2, 8, 2, 16, 256), BF16),
        ((8, 16, RES), BF16), ((8, 16, RES), BF16), ((16, 16, 256), BF16), ((16, 16, 256), BF16), ((2, 8, 2, 16, 256), BF16),
        ((8, 2, 16, 256), BF16), ((2, 8, 16, 256), BF16),
        ((32, 16, 128), BF16), ((32, 16, 128), BF16),
        ((16, 32, 128), BF16), ((16, 32, 128), BF16),
        ((32, 16, 128), BF16), ((32, 16, 128), BF16),
        ((2, 8, 16, 256), BF16),
    ]
    swapped = pl.pallas_call(
        kernel,
        out_shape=pltpu.VMEM((8, 16, RES), BF16),
        in_specs=[pl.BlockSpec(memory_space=pltpu.HBM)] * 9,
        out_specs=pl.BlockSpec(memory_space=pltpu.VMEM),
        scratch_shapes=[pltpu.VMEM(shape, kind) for shape, kind in scratch]
        + [pltpu.SemaphoreType.DMA((9,)), pltpu.SemaphoreType.DMA((22,)), pltpu.SemaphoreType.DMA((22,))],
        compiler_params=pltpu.CompilerParams(
            collective_id=0, has_side_effects=True, vmem_limit_bytes=VMEM_LIMIT),
    )(pair, pair_mask, jnp.swapaxes(ab_weight, 1, 2).reshape(2, 32, CH), in_gain.reshape(1, CH), in_bias.reshape(1, CH),
      gate_weight.T, out_weight, hid_gain.reshape(1, 16), hid_bias.reshape(1, 16))
    return jnp.swapaxes(swapped, 0, 1)


def solution(mesh):
    placed = (
        P("ch", "dap", None),
        P("dap", None),
        P(),
        P(),
        P(None, None, "ch"),
        P("ch"),
        P("ch"),
        P("ch", None),
        P(None, "ch"),
    )
    return jax.shard_map(
        body, mesh=mesh, in_specs=placed, out_specs=P("ch", "dap", None), check_vma=False
    )
```

```python
import jax
import jax.numpy as jnp
from jax import lax
from jax.experimental import pallas as pl
from jax.experimental.pallas import tpu as pltpu
from jax.sharding import PartitionSpec as P

CH = 128
RES = 512
EPS = 1e-05
VMEM_LIMIT = 62 * 1024 * 1024
MESH = pl.DeviceIdType.MESH
F32 = jnp.float32
BF16 = jnp.bfloat16


def nt(a, b):
    return lax.dot_general(a, b, (((1,), (1,)), ((), ())), preferred_element_type=F32)


def nn(a, b):
    return lax.dot_general(a, b, (((1,), (0,)), ((), ())), preferred_element_type=F32)


def iota(shape, dim):
    return lax.broadcasted_iota(jnp.int32, shape, dim)


def bits(value, low, count):
    return lax.shift_right_logical(value, low) & ((1 << count) - 1)


def sigmoid(x):
    return 1.0 / (1.0 + jnp.exp(-x))


def norm(values, gain, bias):
    mean = jnp.sum(values, 0, keepdims=True) * (1.0 / CH)
    square = jnp.sum(values * values, 0, keepdims=True) * (1.0 / CH)
    var = square - mean * mean
    return (values - mean) * lax.rsqrt(var + EPS) * gain + bias


def each(first, last, body):
    def step(k, carry):
        body(k)
        return carry
    lax.fori_loop(first, last, step, 0, unroll=True)


def far(n, top):
    return top + lax.div(n + 1, 2) * (1 - 2 * lax.rem(n, 2))


def kernel(pair_in, mask_in, ab_in, gain_in, bias_in, gate_in, out_in, hid_gain_in, hid_bias_in, out,
           pair, mask, wsend, gain, bias, hid_gain, hid_bias,
           work, zsend, zrecv, wrecv, hsend, hrecv, msend, mrecv,
           rsend, rrecv, rrows, rbuf, lsend, lmid, lrows, lrecv, lbuf, tsend, t1, t2send, t2, gsend, g1, g2send, g2, usend,
           lsem, ssem, rsem):
    div, rem = lax.div, lax.rem
    dap = lax.axis_index("dap")
    ch = lax.axis_index("ch")
    x, z_hi = div(ch, 2), rem(ch, 2)
    y, z_lo, core = div(dap, 8), rem(div(dap, 2), 4), rem(dap, 2)
    z = z_hi * 4 + z_lo
    b = y * 2 + core
    e_lo, s = rem(z + 2, 4), div(rem(z + 6, 8), 4)
    e_ch = 2 * x + s
    u = rem(x, 2)
    f = e_lo * 4 + div(x, 2) * 2 + s
    e = u * 16 + f

    def place(x2, z2):
        return ((y * 4 + rem(z2, 4)) * 2 + core, x2 * 2 + div(z2, 4))

    def f_of(x2, z2):
        return rem(z2 + 2, 4) * 4 + div(x2, 2) * 2 + div(rem(z2 + 6, 8), 4)

    def dev_y(y2):
        return ((y2 * 4 + z_lo) * 2 + core, ch)

    sibling = (dap + 1 - 2 * core, ch)

    def send(src, dst, sem, device):
        pltpu.make_async_remote_copy(
            src_ref=src, dst_ref=dst, send_sem=ssem.at[sem], recv_sem=rsem.at[sem],
            device_id=device, device_id_type=MESH).start()

    def wait_in(ref, sem):
        pltpu.make_async_copy(ref, ref, rsem.at[sem]).wait()

    def wait_out(ref, sem):
        pltpu.make_async_copy(ref, ref, ssem.at[sem]).wait()

    def to_x(k):
        return rem(x + far(k, 2), 4)

    def to_y(k):
        return rem(y + far(k, 4), 8)

    def to_z(k):
        return rem(z + far(k, 4), 8)

    loads = [
        pltpu.make_async_copy(source, target, lsem.at[i]) for i, (source, target) in enumerate((
            (pair_in, pair), (mask_in, mask), (ab_in, wsend.at[:, pl.ds(0, 32)]),
            (gate_in, wsend.at[0, pl.ds(32, 16)]), (out_in, wsend.at[1, pl.ds(32, 16)]),
            (gain_in, gain), (bias_in, bias), (hid_gain_in, hid_gain), (hid_bias_in, hid_bias)))
    ]
    for load in loads:
        load.start()

    barrier = pltpu.get_barrier_semaphore()

    def greet(device):
        pl.semaphore_signal(barrier, inc=1, device_id=device, device_id_type=MESH)

    greet(dev_y(rem(y + 4, 8)))
    each(0, 8, lambda k: greet(place(to_x(div(k, 2)), rem(z + 2 + 4 * rem(k, 2), 8))))
    each(1, 7, lambda k: greet(dev_y(to_y(k))))
    each(0, 3, lambda k: greet(place(to_x(k), z)))
    each(0, 2, lambda k: greet(place(x, rem(z + 1 + 6 * k, 8))))
    greet(sibling)

    for load in loads:
        load.wait()
    for kc in range(4):
        work[kc, pl.ds(0, 128), :] = pair[:, :, pl.ds(kc * 128, 128)].astype(F32).reshape(128, 128)
    for kc in range(4):
        for r in range(8):
            zsend[r, :, pl.ds(kc * 128, 128)] = work[kc, pl.ds(r, 16, stride=8), :].astype(BF16)
    own_mask = mask[pl.ds(ch, 1), :].astype(F32)
    for kc in range(4):
        msend[pl.ds(kc, 1), :] = own_mask[:, kc * 128:kc * 128 + 128]

    pl.semaphore_wait(barrier, 21)

    def first(k):
        x2, s2 = to_x(div(k, 2)), rem(s + k, 2)
        send(zsend.at[x2 * 2 + s2], zrecv.at[ch], 0, place(x2, rem(z_lo + 2 + 4 * s2, 8)))

    z6 = 4 * (1 - z_hi) + 2 * (1 - div(z_lo, 2)) + rem(z_lo, 2)
    crossed = x * 2 + 1 - z_hi

    def along_x(src, dst, sem):
        each(0, 3, lambda k: send(src, dst, sem, place(to_x(k), z)))

    each(0, 4, lambda k: send(wsend.at[core, pl.ds(0, 32)], wrecv.at[ch, core, pl.ds(0, 32)], 2, place(to_x(k), z6)))
    along_x(wsend.at[core, pl.ds(0, 32)], wrecv.at[ch, core, pl.ds(0, 32)], 2)
    each(0, 8, first)
    each(0, 4, lambda k: send(wsend.at[core, pl.ds(32, 16)], wrecv.at[ch, core, pl.ds(32, 16)], 3, place(to_x(k), z6)))
    along_x(wsend.at[core, pl.ds(32, 16)], wrecv.at[ch, core, pl.ds(32, 16)], 3)
    send(msend, mrecv, 13, place(x, rem(z_lo + 2 + 4 * z_hi, 8)))
    wrecv[ch, core] = wsend[core]

    eye = iota((128, 128), 0) == iota((128, 128), 1)
    gain_col = jnp.sum(jnp.where(eye, gain[...], 0.0), 1, keepdims=True)
    bias_col = jnp.sum(jnp.where(eye, bias[...], 0.0), 1, keepdims=True)
    hsend[...] = jnp.zeros((1, 128), F32)
    hsend[:, pl.ds(0, 16)] = hid_gain[...]
    hsend[:, pl.ds(16, 16)] = hid_bias[...]

    wait_in(wrecv.at[pl.ds(0, 7), 0, pl.ds(0, 32)], 2)
    send(wrecv.at[:, core, pl.ds(0, 32)], wrecv.at[:, core, pl.ds(0, 32)], 17, sibling)
    wait_in(zrecv, 0)
    zn = norm(zrecv[...].astype(F32).reshape(128, RES), gain_col, bias_col).astype(BF16)
    wait_in(mrecv, 13)
    masking = jnp.concatenate([mrecv[pl.ds(kc, 1), :] for kc in range(4)], axis=1)
    wait_in(wrecv.at[:, 0, pl.ds(0, 32)], 17)

    def operand(side):
        opened = sigmoid(nn(wrecv[:, side, pl.ds(0, 16)].reshape(128, 128), zn))
        value = nn(wrecv[:, side, pl.ds(16, 16)].reshape(128, 128), zn)
        return opened * value * masking

    def swap_f(sent, received, sem):
        def one(k):
            x2, z2 = rem(x + 2 * rem(k + 1, 2), 4), to_z(div(k, 2))
            send(sent.at[f_of(x2, z2)], received.at[f], sem, place(x2, z2))
        each(0, 15, one)
        received[f] = sent[f]

    def swap_y(sent, slot, sem):
        each(0, 7, lambda k: send(sent.at[to_y(k)], slot, sem, dev_y(to_y(k))))

    right = operand(1).reshape(16, 8, RES)

    def swap_right(kh):
        at = kh * 256
        rsend[kh] = jnp.concatenate([right[:, :, at:at + 128], right[:, :, at + 128:at + 256]], axis=1).astype(BF16)
        swap_f(rsend.at[kh], rrecv.at[kh], 4 + 15 * kh)

    swap_right(0)
    swap_right(1)
    left = operand(0)
    for lc in range(4):
        work[lc, pl.ds(0, 128), :] = left[:, lc * 128:lc * 128 + 128]
    for kh in range(2):
        for lc in range(2):
            for h in range(8):
                lsend[kh, h, :, pl.ds(lc * 128, 128)] = work[kh * 2 + lc, pl.ds(h, 16, stride=8), :].astype(BF16)
        swap_y(lsend.at[kh], lmid.at[kh, y], 14 + 8 * kh)
        lmid[kh, y] = lsend[kh, y]
    hrecv[ch] = hsend[...]

    wait_in(wrecv.at[pl.ds(0, 7), 0, pl.ds(32, 16)], 3)
    send(wrecv.at[:, core, pl.ds(32, 16)], wrecv.at[:, core, pl.ds(32, 16)], 1, sibling)
    wait_in(wrecv.at[:, 0, pl.ds(32, 16)], 1)
    gate = sigmoid(nn(wrecv[:, 0, pl.ds(32, 16)].reshape(128, 128), zn)).T.reshape(8, 4, 2, 8, 128)
    for yy in range(8):
        for cc in range(2):
            gsend[yy * 2 + cc] = gate[yy, :, cc].reshape(32, 128).astype(BF16)

    def gate_b(k):
        y2, core2 = to_y(div(k, 2)), rem(core + 1 + k, 2)
        send(gsend.at[y2 * 2 + core2], g1.at[b], 5, ((y2 * 4 + z_lo) * 2 + core2, ch))

    each(0, 15, gate_b)
    g1[b] = gsend[b]

    each(0, 4, lambda k: send(hsend, hrecv.at[ch], 16, place(to_x(k), z6)))
    along_x(hsend, hrecv.at[ch], 16)

    def spread_right(kh):
        wait_in(rrecv.at[kh, pl.ds(0, 15)], 4 + 15 * kh)
        work[kh, pl.ds(0, 256), :] = rrecv[kh].astype(F32).reshape(256, 128)
        for h in range(8):
            for lc in range(2):
                rrows[kh, h, :, pl.ds(lc * 128, 128)] = work[kh, pl.ds(lc * 8 + h, 16, stride=16), :].astype(BF16)
        if kh == 1:
            each(0, 8, lambda k: send(rrows.at[1, to_y(k)], rbuf.at[1, y, u], 20, (dev_y(to_y(k))[0], ch + 2 - 4 * u)))
        swap_y(rrows.at[kh], rbuf.at[kh, y, u], 11 + 9 * kh)
        rbuf[kh, y, u] = rrows[kh, y]

    def spread_left(kh):
        wait_in(lmid.at[kh, pl.ds(0, 7)], 14 + 8 * kh)
        for lc in range(2):
            work[lc, pl.ds(256, 128), :] = lmid[kh, :, :, pl.ds(lc * 128, 128)].astype(F32).reshape(128, 128)
        for g in range(16):
            lrows[kh, g] = jnp.concatenate(
                [work[lc, pl.ds(256 + g, 8, stride=16), :] for lc in range(2)], axis=0).astype(BF16)
        swap_f(lrows.at[kh], lrecv.at[kh], 6 + 17 * kh)

    spread_left(0)
    spread_right(0)
    spread_left(1)
    spread_right(1)

    wait_in(rbuf.at[0, pl.ds(0, 7), 0], 11)
    send(rbuf.at[0, :, u], rbuf.at[0, :, u], 15, place(x + 1 - 2 * u, z))

    wout_t = nt(eye.astype(BF16), wrecv[:, 1, pl.ds(32, 16)].reshape(128, 128)).astype(BF16)
    wait_in(hrecv.at[pl.ds(0, 7)], 16)
    at_gain = iota((8, 16, 128), 1) == iota((8, 16, 128), 2)
    at_bias = iota((8, 16, 128), 1) + 16 == iota((8, 16, 128), 2)

    def column(where):
        col = jnp.sum(jnp.where(where, hrecv[...], 0.0), 2, keepdims=True)
        return jnp.broadcast_to(col, (8, 16, 128)).reshape(128, 128)

    hg, hb = column(at_gain), column(at_bias)
    lane = iota((256, 256), 0)
    natural = (bits(lane, 5, 2) * 64 + bits(lane, 2, 2) * 16 + bits(lane, 4, 1) * 8
               + bits(lane, 1, 1) * 4 + bits(lane, 7, 1) * 2 + bits(lane, 0, 1))
    perm = (natural == iota((256, 256), 1)).astype(BF16)

    for kh in range(2):
        wait_in(lrecv.at[kh, pl.ds(0, 15)], 6 + 17 * kh)
        work[2 + kh, pl.ds(0, 256), :] = lrecv[kh].astype(F32).reshape(256, 128)
        for yy in range(8):
            for lc in range(2):
                lbuf[kh, yy, core, :, pl.ds(lc * 128, 128)] = work[2 + kh, pl.ds(lc * 8 + yy, 16, stride=16), :].astype(BF16)
        send(lbuf.at[kh, :, core], lbuf.at[kh, :, core], 12 + 12 * kh, sibling)
    wait_in(rbuf.at[0, :, 0], 15)
    wait_in(rrecv.at[:, pl.ds(0, 15)], 20)
    wait_in(lbuf.at[0, :, 0], 12)
    wait_in(lbuf.at[1, :, 0], 24)
    tri = nt(rbuf[0].reshape(256, 256), lbuf[0].reshape(256, 256)) + nt(rbuf[1].reshape(256, 256), lbuf[1].reshape(256, 256))
    tsend[...] = tri.astype(BF16).reshape(8, 2, 16, 256)

    for v in range(2):
        each(0, 7, lambda k: send(tsend.at[to_y(k), v], t1.at[v, y], 8 + v, dev_y(to_y(k))))
        t1[v, y] = tsend[y, v]

    wait_in(g1.at[pl.ds(0, 15)], 5)
    work[2, :, :] = g1[...].astype(F32).reshape(512, 128)
    for j in range(32):
        lo, high, parity, low = j % 16 // 4, j % 4 // 2, j // 16, j % 2
        g2send[j] = work[2, pl.ds(lo * 8 + high * 4 + parity * 2 + low, 16, stride=32), :].astype(BF16)

    def gate_e(k):
        x2, z2 = to_x(rem(k, 4)), to_z(div(k, 4))
        send(g2send.at[rem(x2, 2) * 16 + f_of(x2, z2)], g2.at[e], 7, place(x2, z2))

    each(0, 31, gate_e)
    g2[e] = g2send[e]

    for v in range(2):
        wait_in(t1.at[v, pl.ds(0, 7)], 8 + v)
        for lc in range(2):
            work[lc, pl.ds(0, 128), :] = t1[v, :, :, pl.ds(lc * 128, 128)].astype(F32).reshape(128, 128)
        for j in range(16):
            t2send[v * 16 + j] = jnp.concatenate(
                [work[lc, pl.ds(j, 8, stride=16), :] for lc in range(2)], axis=0).astype(BF16)
        w = rem(u + v, 2)

        def forward(k):
            x2, z2 = rem(x + 2 - w + rem(k, 2) * (4 * w - 2), 4), to_z(div(k, 2))
            send(t2send.at[v * 16 + f_of(x2, z2)], t2.at[e], 10, place(x2, z2))

        each(0, 15, forward)

        @pl.when(w == 1)
        def _():
            forward(15)

        @pl.when(w == 0)
        def _():
            t2[e] = t2send[v * 16 + f]

    wait_in(g2.at[pl.ds(0, 31)], 7)
    work[2, :, :] = g2[...].astype(F32).reshape(512, 128)
    gate_t = jnp.concatenate(
        [work[2, pl.ds(uu * 256 + bb, 16, stride=16), :] for uu in range(2) for bb in range(16)], axis=0).T

    wait_in(t2.at[pl.ds(0, 31)], 10)
    tiles = t2[...].astype(F32).reshape(2, 16, 2, 8, 128)
    for lt in range(2):
        parts = []
        for uu in range(2):
            tri_ln = norm(tiles[uu, :, lt].reshape(128, 128), hg, hb).astype(BF16)
            at = uu * 256 + lt * 128
            parts.append((nn(wout_t, tri_ln) * gate_t[:, at:at + 128]).astype(BF16))
        update = nn(jnp.concatenate(parts, axis=1), perm)
        usend[lt] = update.astype(BF16).reshape(8, 16, 256)

        def last(k):
            x2, half = to_x(div(k, 2)), rem(z_hi + k, 2)
            send(usend.at[lt, x2 * 2 + half], out.at[e_ch, :, pl.ds(lt * 256, 256)], 18, place(x2, e_lo + 4 * half))

        each(0, 8, last)

    wait_out(zsend, 0)
    wait_out(wrecv.at[:, 0, pl.ds(32, 16)], 1)
    wait_out(wrecv.at[pl.ds(0, 7), 0, pl.ds(0, 32)], 2)
    wait_out(wrecv.at[pl.ds(0, 7), 0, pl.ds(32, 16)], 3)
    wait_out(rsend.at[0, pl.ds(0, 15)], 4)
    wait_out(rsend.at[1, pl.ds(0, 15)], 19)
    wait_out(lsend.at[0, pl.ds(0, 7)], 14)
    wait_out(lsend.at[1, pl.ds(0, 7)], 22)
    wait_out(gsend.at[pl.ds(0, 15)], 5)
    wait_out(lrows.at[0, pl.ds(0, 15)], 6)
    wait_out(lrows.at[1, pl.ds(0, 15)], 23)
    wait_out(g2send.at[pl.ds(0, 31)], 7)
    wait_out(t1.at[0, pl.ds(0, 7)], 8)
    wait_out(t1.at[1, pl.ds(0, 7)], 9)
    wait_out(t2send.at[pl.ds(0, 31)], 10)
    wait_out(rrows.at[0, pl.ds(0, 7)], 11)
    wait_out(rrecv.at[:, pl.ds(0, 15)], 20)
    wait_out(lbuf.at[0, :, 0], 12)
    wait_out(lbuf.at[1, :, 0], 24)
    wait_out(msend, 13)
    wait_out(rbuf.at[0, :, 0], 15)
    wait_out(hrecv.at[pl.ds(0, 7)], 16)
    wait_out(wrecv.at[:, 0, pl.ds(0, 32)], 17)
    wait_out(usend, 18)
    wait_in(out, 18)


def body(pair, pair_mask, in_gain, in_bias, ab_weight, hid_gain, hid_bias, out_weight, gate_weight):
    rows = pair.shape[1]
    scratch = [
        ((16, rows, RES), BF16), ((rows, RES), jnp.int32), ((2, 48, 128), BF16),
        ((1, CH), F32), ((1, CH), F32), ((1, 16), F32), ((1, 16), F32),
        ((4, 512, 128), F32),
        ((8, 16, RES), BF16), ((8, 16, RES), BF16),
        ((8, 2, 48, 128), BF16),
        ((1, 128), F32), ((8, 1, 128), F32),
        ((8, 128), F32), ((8, 128), F32),
        ((2, 16, 16, 128), BF16), ((2, 16, 16, 128), BF16), ((2, 8, 16, 256), BF16), ((2, 8, 2, 16, 256), BF16),
        ((2, 8, 16, 256), BF16), ((2, 8, 16, 256), BF16), ((2, 16, 16, 128), BF16), ((2, 16, 16, 128), BF16), ((2, 8, 2, 16, 256), BF16),
        ((8, 2, 16, 256), BF16), ((2, 8, 16, 256), BF16),
        ((32, 16, 128), BF16), ((32, 16, 128), BF16),
        ((16, 32, 128), BF16), ((16, 32, 128), BF16),
        ((32, 16, 128), BF16), ((32, 16, 128), BF16),
        ((2, 8, 16, 256), BF16),
    ]
    swapped = pl.pallas_call(
        kernel,
        out_shape=pltpu.VMEM((8, 16, RES), BF16),
        in_specs=[pl.BlockSpec(memory_space=pltpu.HBM)] * 9,
        out_specs=pl.BlockSpec(memory_space=pltpu.VMEM),
        scratch_shapes=[pltpu.VMEM(shape, kind) for shape, kind in scratch]
        + [pltpu.SemaphoreType.DMA((9,)), pltpu.SemaphoreType.DMA((25,)), pltpu.SemaphoreType.DMA((25,))],
        compiler_params=pltpu.CompilerParams(
            collective_id=0, has_side_effects=True, vmem_limit_bytes=VMEM_LIMIT),
    )(pair, pair_mask, jnp.swapaxes(ab_weight, 1, 2).reshape(2, 32, CH), in_gain.reshape(1, CH), in_bias.reshape(1, CH),
      gate_weight.T, out_weight, hid_gain.reshape(1, 16), hid_bias.reshape(1, 16))
    return jnp.swapaxes(swapped, 0, 1)


def solution(mesh):
    placed = (
        P("ch", "dap", None),
        P("dap", None),
        P(),
        P(),
        P(None, None, "ch"),
        P("ch"),
        P("ch"),
        P("ch", None),
        P(None, "ch"),
    )
    return jax.shard_map(
        body, mesh=mesh, in_specs=placed, out_specs=P("ch", "dap", None), check_vma=False
    )
```
